256 devices in a mesh: feat: 2 (over core), dom: 128 (over z, y, x).
Axes of the slice: x: 4, y: 4, z: 8, core: 2. Of those that a mesh axis runs over, the one named last changes fastest.
Arguments:
- features: bfloat16 [131072, 1024], P('dom', 'feat'), may hold values from -6 to 6
- tile_weight: bfloat16 [16384, 128, 128], P('dom'), may hold values from 0 to 0.029907227
- tile_dst: int32 [16384], P('dom'), may hold values from 0 to 127
- tile_src: int32 [16384], P('dom'), may hold values from 0 to 7
- tile_rows: int32 [16384], P('dom'), may hold values from 1 to 128
- w_self1: bfloat16 [1024, 256], P('feat'), may hold values from -0.1875 to 0.1875
- neighbour_weight_first: bfloat16 [1024, 256], P('feat'), may hold values from -0.1875 to 0.1875
- send_list: int32 [128, 128, 8], replicated, may hold values from 0 to 127
- send_count: int32 [128, 128], replicated, may hold values from 1 to 8
- adj_two: bfloat16 [8192, 1152], P('dom'), may hold values from 0 to 0.0049743652
- w_self2: bfloat16 [256, 172], replicated, may hold values from -0.375 to 0.375
- w_neigh2: bfloat16 [256, 172], replicated, may hold values from -0.375 to 0.375
Outputs:
- logits: float32 [8192, 172], P('dom')
The draws below stay inside these ranges and needn't reach their ends.
Inputs may be any that keep to these rules, and one draw needn't show every extreme that they name: `send_list`: every send list slot names a local hidden row of the sender.
All inputs are finite; a program needn't handle non-finite values.
Results may differ from the reference program's by a relative error of at most 0.0012.
The reference program's roundings to bfloat16 on the way count: a program that leaves them out, or rounds other values in their place, can miss the bound.
Values may be sent and summed in bfloat16 or wider, within the bound.
A program may use at most 128 MiB of HBM per device.

```python
import math
import jax
import jax.numpy as jnp
import numpy as np
from jax import lax

F = 1024
H = 256
C = 172
TILE = 128
HID_DEV = 128
ROWS_DEV = 1024
TILES = 128
OUT_DEV = 64
SEND_MAX = 8
N_NODES = 131072
N_TILES = 16384
BATCH = 8192
POOL = 1152
N_DOM = 128


def plant(drawn, stream_key, least, high):
    longest = drawn.shape.index(max(drawn.shape))
    spots = []
    for shift in (0, 1):
        where = [jax.random.randint(jax.random.fold_in(stream_key, axis), (), 0, length) for axis, length in enumerate(drawn.shape)]
        where[longest] = (where[longest] + shift) % drawn.shape[longest]
        spots.append(tuple(where))
    return drawn.at[spots[0]].set(least).at[spots[1]].set(high)


def block_scale(rng, extent, shards, low, top_value):
    loudness = 1.0
    for axis_at, blocks in shards:
        steps = jax.random.uniform(jax.random.fold_in(jax.random.fold_in(rng, 6), axis_at), (blocks,), jnp.float32, low / len(shards), top_value / len(shards))
        loudness = loudness * jnp.repeat(jnp.exp(steps), extent[axis_at] // blocks).reshape((-1,) + (1,) * (len(extent) - 1 - axis_at))
    return loudness


def rank_bounds(number_of, skew):
    portions = [(1 << 20) // math.isqrt(grade ** skew) + 1 for grade in range(1, number_of + 1)]
    scale = 1 + sum(portions) // (1 << 30)
    return np.cumsum(np.array([max(1, weight // scale) for weight in portions]))


def ranked_ids(own_key, dims, number_of, slope):
    table = rank_bounds(number_of, slope)
    pick = jax.random.randint(jax.random.fold_in(own_key, 1), dims, 0, int(table[number_of - 1]))
    standing = jnp.searchsorted(jnp.asarray(table, jnp.int32), pick, side="right")
    return jax.random.permutation(jax.random.fold_in(own_key, 2), number_of)[standing].astype(jnp.int32)


def normal_values(rng, extent, width, most, split=(), kind=jnp.bfloat16):
    values = jax.random.normal(rng, extent, jnp.float32) * width
    if len(split) > 0:
        values = block_scale(rng, extent, split, -0.22, 0.18) * values
    return jnp.clip(values, min=-most, max=most).astype(kind)


def setup_inputs(seed: int = 0) -> dict:
    arg_keys = jax.random.split(jax.random.key(seed), 13)
    return {
        "features": normal_values(arg_keys[0], (N_NODES, F), 1.0, 6.0, ((0, 128), (1, 2))),
        "tile_weight": jnp.clip(0.029907227 * jax.random.uniform(arg_keys[1], (N_TILES, TILE, TILE), jnp.float32) ** block_scale(arg_keys[1], (N_TILES, TILE, TILE), ((0, 128),), -0.2, 0.2), 0.0, 0.029907227).astype(jnp.bfloat16),
        "tile_dst": plant(ranked_ids(arg_keys[2], (N_TILES,), N_DOM, 2), jax.random.fold_in(arg_keys[2], 3), 0, N_DOM - 1).astype(jnp.int32),
        "tile_src": plant(jax.random.randint(arg_keys[3], (N_TILES,), 0, ROWS_DEV // TILE), jax.random.fold_in(arg_keys[3], 1), 0, (ROWS_DEV // TILE) - 1).astype(jnp.int32),
        "tile_rows": plant(jax.random.randint(arg_keys[4], (N_TILES,), 1, TILE + 1), jax.random.fold_in(arg_keys[4], 1), 1, TILE).astype(jnp.int32),
        "w_self1": normal_values(arg_keys[5], (F, H), F ** -0.5, 0.1875, ((0, 2),)),
        "neighbour_weight_first": normal_values(arg_keys[6], (F, H), F ** -0.5, 0.1875, ((0, 2),)),
        "send_list": plant(jax.random.randint(arg_keys[7], (N_DOM, N_DOM, SEND_MAX), 0, HID_DEV), jax.random.fold_in(arg_keys[7], 1), 0, HID_DEV - 1).astype(jnp.int32),
        "send_count": plant(jax.random.randint(arg_keys[8], (N_DOM, N_DOM), 1, SEND_MAX + 1), jax.random.fold_in(arg_keys[8], 1), 1, SEND_MAX).astype(jnp.int32),
        "adj_two": jnp.clip(0.0049743652 * jax.random.uniform(arg_keys[9], (BATCH, POOL), jnp.float32) ** block_scale(arg_keys[9], (BATCH, POOL), ((0, 128),), -0.2, 0.2), 0.0, 0.0049743652).astype(jnp.bfloat16),
        "w_self2": normal_values(arg_keys[10], (H, C), H ** -0.5, 0.375),
        "w_neigh2": normal_values(arg_keys[11], (H, C), H ** -0.5, 0.375),
    }


def reference(features, tile_weight, tile_dst, tile_src, tile_rows, w_self1, neighbour_weight_first, send_list, send_count, adj_two, w_self2, w_neigh2):
    blocks_all = features.reshape(N_DOM, ROWS_DEV // TILE, TILE, F)
    weight_pieces = tile_weight.reshape(N_DOM, TILES, TILE, TILE)
    dst_parts = tile_dst.reshape(N_DOM, TILES)
    src_parts = tile_src.reshape(N_DOM, TILES)
    rows_parts = tile_rows.reshape(N_DOM, TILES)
    row_indices = jnp.arange(TILE, dtype=jnp.int32)
    block_ids = jnp.arange(N_DOM, dtype=jnp.int32)

    def partition(total, index):
        blocks = blocks_all[index]
        valid = row_indices[None, :, None] < rows_parts[index][:, None, None]
        masked_features = jnp.where(valid, weight_pieces[index], jnp.zeros_like(weight_pieces[index]))
        source_nodes = blocks[src_parts[index]]
        collected_rows = jnp.einsum('zvx,zxm->zvm', masked_features.astype(jnp.float32), source_nodes.astype(jnp.float32)).astype(jnp.bfloat16)
        neighbour_rows = jnp.einsum('kys,sj->kyj', collected_rows.astype(jnp.float32), neighbour_weight_first.astype(jnp.float32))
        onehot = (dst_parts[index][:, None] == block_ids[None, :]).astype(jnp.float32)
        term = jnp.einsum('tb,trh->brh', onehot, neighbour_rows, precision=lax.Precision.HIGHEST)
        return total + term, 0

    start = jnp.zeros((N_DOM, TILE, H), jnp.float32)
    neigh_sum, unused = lax.scan(partition, start, jnp.arange(N_DOM, dtype=jnp.int32))
    own = blocks_all[:, 0].reshape(N_DOM * TILE, F)
    pre = jnp.dot(own, w_self1, preferred_element_type=jnp.float32) + neigh_sum.reshape(N_DOM * TILE, H)
    hidden = jnp.maximum(pre, 0.0).astype(jnp.bfloat16)
    hidden_parts = hidden.reshape(N_DOM, HID_DEV, H)
    slots = jnp.arange(SEND_MAX, dtype=jnp.int32)

    def second(receiver):
        lists = send_list[:, receiver, :]
        counts = send_count[:, receiver]
        flat = (block_ids[:, None] * HID_DEV + lists).reshape(N_DOM * SEND_MAX)
        rows = hidden[flat].reshape(N_DOM, SEND_MAX, H)
        rows = jnp.where((slots[None, :] < counts[:, None])[:, :, None], rows, jnp.zeros_like(rows))
        pool = jnp.concatenate([hidden_parts[receiver], rows.reshape(N_DOM * SEND_MAX, H)], axis=0)
        adjacency = lax.dynamic_slice_in_dim(adj_two, receiver * OUT_DEV, OUT_DEV, 0)
        neighbour_mean = jnp.dot(adjacency, pool, preferred_element_type=jnp.float32).astype(jnp.bfloat16)
        selfrows = hidden_parts[receiver][:OUT_DEV]
        return jnp.dot(selfrows, w_self2, preferred_element_type=jnp.float32) + jnp.dot(neighbour_mean, w_neigh2, preferred_element_type=jnp.float32)

    logits = lax.map(second, jnp.arange(N_DOM, dtype=jnp.int32))
    return logits.reshape(N_DOM * OUT_DEV, C)
```

```python
import functools

import jax
import jax.numpy as jnp
import numpy as np
from jax import lax
from jax.experimental import pallas as pl
from jax.experimental.pallas import tpu as pltpu
from jax.sharding import PartitionSpec as P

DIMS = {128: (4, 4, 8), 16: (4, 2, 2)}
SHARES = ((0, 24), (24, 24), (48, 16))
ORDERS = ((0, 1, 2), (1, 0, 2), (2, 0, 1))
GROUP = 4
VMEM_LIMIT = 56 * 1024 * 1024
MESH = pl.DeviceIdType.MESH


def bits_of(count):
    return count.bit_length() - 1


def steps_of(parts, share):
    dims = DIMS[parts]
    return [(axis, i) for axis in ORDERS[share] for i in range(bits_of(dims[axis]))]


def chunk_of(parts):
    return parts // 8


def packed_from(parts):
    return 8 if parts >= 128 else 2


@functools.lru_cache(maxsize=None)
def slot_table(parts):
    nx, ny, nz = DIMS[parts]
    table = np.zeros((2, len(SHARES), parts), np.int32)
    for f in range(2):
        for share in range(len(SHARES)):
            for b in range(parts):
                coords = (b % nx, b // nx % ny, b // (nx * ny))
                slot = 0
                for axis, i in steps_of(parts, share):
                    n = DIMS[parts][axis]
                    c = (coords[axis] - f) % n
                    slot = slot * 2 + ((c ^ (c >> 1)) >> i & 1)
                table[f, share, b] = slot
    return table


def partner_of(parts, me, f, axis, i):
    nx, ny, nz = DIMS[parts]
    coords = [me % nx, me // nx % ny, me // (nx * ny)]
    n = DIMS[parts][axis]
    block = 2 ** (i + 1)
    c = (coords[axis] - f + n) % n
    c = c - c % block + (block - 1 - c % block)
    coords[axis] = (c + f) % n
    return (coords[2] * ny + coords[1]) * nx + coords[0]


def swap_kernel(x_ref, wn_ref, ws_ref, xo_ref, wno_ref, wso_ref, send, recv):
    other = 1 - lax.axis_index("feat")
    barrier = pltpu.get_barrier_semaphore()
    pl.semaphore_signal(barrier, inc=1, device_id={"feat": other}, device_id_type=MESH)
    pl.semaphore_wait(barrier, 1)
    copies = []
    for k, (a, b) in enumerate(((x_ref, xo_ref), (wn_ref, wno_ref), (ws_ref, wso_ref))):
        copy = pltpu.make_async_remote_copy(
            src_ref=a,
            dst_ref=b,
            send_sem=send.at[k],
            recv_sem=recv.at[k],
            device_id={"feat": other},
            device_id_type=MESH,
        )
        copy.start()
        copies.append(copy)
    for copy in copies:
        copy.wait()


def swap(features, wn, ws):
    anywhere = pl.BlockSpec(memory_space=pl.ANY)
    return pl.pallas_call(
        swap_kernel,
        out_shape=[jax.ShapeDtypeStruct(a.shape, a.dtype) for a in (features, wn, ws)],
        in_specs=[anywhere] * 3,
        out_specs=[anywhere] * 3,
        scratch_shapes=[pltpu.SemaphoreType.DMA((3,)), pltpu.SemaphoreType.DMA((3,))],
        compiler_params=pltpu.CompilerParams(collective_id=0, has_side_effects=True),
        name="swap_halves",
    )(features, wn, ws)


def encode(load, count, rows, out, peak, inv):
    def largest(j, carry):
        v = jnp.abs(load(j))
        half = v.shape[1] // 2
        peak[pl.ds(j, 1), :] = jnp.max(jnp.maximum(v[:, :half], v[:, half:]), axis=0, keepdims=True)
        return carry

    lax.fori_loop(0, count, largest, 0, unroll=True)
    top = jnp.maximum(peak[:count, :], 1e-30)
    code = jnp.ceil(jnp.log2(top) * 256.0) + 1.0
    out[count * rows :, :] = code.astype(jnp.int32)
    inv[:count, :] = jnp.exp2(code * (-1.0 / 256.0)) * 32767.0

    def pack(j, carry):
        v = load(j)
        half = v.shape[1] // 2
        s = inv[pl.ds(j, 1), :]
        low = jnp.round(v[:, :half] * s).astype(jnp.int32)
        high = jnp.round(v[:, half:] * s).astype(jnp.int32)
        out[pl.ds(j * rows, rows), :] = jnp.bitwise_or(
            jnp.left_shift(high, 16), jnp.bitwise_and(low, 0xFFFF)
        )
        return carry

    lax.fori_loop(0, count, pack, 0, unroll=True)


def decode_add(src, total, rows, low, high, work, first, scale):
    count = high - low
    code = src[total * rows :, :].astype(jnp.float32)
    scale[:total, :] = jnp.exp2(code * (1.0 / 256.0)) * (1.0 / 32767.0)

    def add(j, carry):
        word = src[pl.ds((low + j) * rows, rows), :]
        s = scale[pl.ds(low + j, 1), :]
        a = jnp.right_shift(jnp.left_shift(word, 16), 16).astype(jnp.float32) * s
        b = jnp.right_shift(word, 16).astype(jnp.float32) * s
        half = a.shape[1]
        work[first + low + j, :, :half] += a
        work[first + low + j, :, half:] += b
        return carry

    lax.fori_loop(0, count, add, 0, unroll=True)


def first_layer_kernel(parts, *refs):
    (where, table, dst, src, limit, xa, xb, wa, wb, sa, sb, tiles) = refs[:12]
    keeps, messages, own_out = refs[12:15], refs[15:18], refs[18]
    accs, sends = refs[19:22], refs[22:25]
    order, count, gathered_a, gathered_b, peak, inv, sem = refs[25:]
    f, me = where[0], where[1]
    n_tiles, rows, size = tiles.shape
    blocks = xa.shape[0] // size
    half = parts // 2

    def clear(j, carry):
        for acc in accs:
            acc[j] = jnp.zeros(acc.shape[1:], jnp.float32)
        return carry

    lax.fori_loop(0, parts, clear, 0, unroll=4)
    for s in range(blocks):
        count[s] = 0

    def place(t, carry):
        s = src[t]
        at = count[s]
        order[s, at] = t
        count[s] = at + 1
        return carry

    lax.fori_loop(0, n_tiles, place, 0)

    mine = pl.ds(pl.multiple_of(f * rows, rows), rows)
    own_out[...] = jnp.dot(xa[mine, :], sa[...], preferred_element_type=jnp.float32) + jnp.dot(
        xb[mine, :], sb[...], preferred_element_type=jnp.float32
    )
    row_ids = lax.broadcasted_iota(jnp.int32, (rows, size), 0) + f * rows
    bases = [table[f, share, me] for share in range(len(SHARES))]

    def block(s, carry):
        n = count[s]
        at_source = pl.ds(pl.multiple_of(s * size, size), size)

        def group(g, inner):
            ids, parts_of = [], []
            for j in range(GROUP):
                k = g * GROUP + j
                valid = k < n
                t = jnp.where(valid, order[s, jnp.minimum(k, n_tiles - 1)], 0)
                ids.append(t)
                bound = jnp.where(valid, limit[t], 0)
                tile = tiles[t]
                parts_of.append(jnp.where(row_ids < bound, tile, jnp.zeros_like(tile)))
            a = jnp.concatenate(parts_of, axis=0)
            gathered_a[...] = jnp.dot(a, xa[at_source, :], preferred_element_type=jnp.float32).astype(
                jnp.bfloat16
            )
            gathered_b[...] = jnp.dot(a, xb[at_source, :], preferred_element_type=jnp.float32).astype(
                jnp.bfloat16
            )
            h = jnp.dot(gathered_a[...], wa[...], preferred_element_type=jnp.float32) + jnp.dot(
                gathered_b[...], wb[...], preferred_element_type=jnp.float32
            )
            for j in range(GROUP):
                d = dst[ids[j]]
                for share, (start, length) in enumerate(SHARES):
                    slot = jnp.bitwise_xor(table[f, share, d], bases[share])
                    at = j * rows + start
                    accs[share][slot] += h[at : at + length, :]
            return inner

        return lax.fori_loop(0, (n + GROUP - 1) // GROUP, group, carry)

    lax.fori_loop(0, blocks, block, 0)

    copies = []
    for share in range(len(SHARES)):
        copy = pltpu.make_async_copy(accs[share].at[pl.ds(0, half)], keeps[share], sem.at[share, 0])
        copy.start()
        copies.append(copy)
    chunk = chunk_of(parts)
    pieces = half // chunk
    for piece in range(pieces):
        for share, (start, length) in enumerate(SHARES):
            acc = accs[share]
            first = half + (pieces - 1 - piece) * chunk
            out = sends[share].at[piece]
            encode(lambda j: acc[first + j], chunk, length, out, peak, inv)
            copy = pltpu.make_async_copy(out, messages[share].at[piece], sem.at[share, 1 + piece])
            copy.start()
            copies.append(copy)
    for copy in copies:
        copy.wait()


def first_layer(parts, where, dst, src, limit, features, other, wn, wn_other, ws, ws_other, tiles):
    n_tiles, size, _ = tiles.shape
    rows = size // 2
    width = wn.shape[1]
    half = parts // 2
    chunk = chunk_of(parts)
    pieces = half // chunk
    anywhere = pl.BlockSpec(memory_space=pl.ANY)
    lengths = [length for _, length in SHARES]
    message = [(pieces, chunk * n + chunk, width // 2) for n in lengths]

    def fixed(shape):
        return pl.BlockSpec(shape, lambda i, where, *rest: (0,) * len(shape), pipeline_mode=pl.Buffered(1))

    grid_spec = pltpu.PrefetchScalarGridSpec(
        num_scalar_prefetch=5,
        grid=(1,),
        in_specs=[fixed(a.shape) for a in (features, other, wn, wn_other, ws, ws_other)]
        + [
            pl.BlockSpec(
                (n_tiles, rows, size), lambda i, where, *rest: (0, where[0], 0), pipeline_mode=pl.Buffered(1)
            )
        ],
        out_specs=[anywhere] * 6 + [fixed((rows, width))],
        scratch_shapes=[pltpu.VMEM((parts, n, width), jnp.float32) for n in lengths]
        + [pltpu.VMEM(shape, jnp.int32) for shape in message]
        + [
            pltpu.SMEM((features.shape[0] // size, n_tiles), jnp.int32),
            pltpu.SMEM((features.shape[0] // size,), jnp.int32),
            pltpu.VMEM((GROUP * rows, features.shape[1]), jnp.bfloat16),
            pltpu.VMEM((GROUP * rows, features.shape[1]), jnp.bfloat16),
            pltpu.VMEM((max(chunk, 8), width // 2), jnp.float32),
            pltpu.VMEM((max(chunk, 8), width // 2), jnp.float32),
            pltpu.SemaphoreType.DMA((len(SHARES), 1 + pieces)),
        ],
    )
    return pl.pallas_call(
        functools.partial(first_layer_kernel, parts),
        grid_spec=grid_spec,
        out_shape=[jax.ShapeDtypeStruct((half, n, width), jnp.float32) for n in lengths]
        + [jax.ShapeDtypeStruct(shape, jnp.int32) for shape in message]
        + [jax.ShapeDtypeStruct((rows, width), jnp.float32)],
        compiler_params=pltpu.CompilerParams(vmem_limit_bytes=VMEM_LIMIT),
        name="first_layer",
    )(
        where,
        jnp.asarray(slot_table(parts)),
        dst,
        src,
        limit,
        features,
        other,
        wn,
        wn_other,
        ws,
        ws_other,
        tiles,
    )


def message_plan(parts):
    plan = []
    count = parts // 2
    while count >= 1:
        size = min(count, chunk_of(parts))
        plan.append((count, size, count // size, count >= packed_from(parts)))
        count //= 2
    return plan


def second_layer_kernel(parts, *refs):
    nx, ny, nz = DIMS[parts]
    plane = nx * ny
    plan = message_plan(parts)
    n_shares = len(SHARES)
    keeps, messages = refs[0:3], refs[3:6]
    own_ref, list_ref, adj_ref, w_self_ref, w_neigh_ref, out_ref = refs[6:12]
    at = 12
    work = refs[at : at + 3]
    at += 3
    receive, outgoing = [], []
    for k in range(len(plan)):
        receive.append(refs[at : at + 3])
        at += 3
    for k in range(len(plan)):
        coded = plan[k][3] and k > 0
        outgoing.append(refs[at : at + 3] if coded else None)
        at += 3 if coded else 0
    (peak, inv, scale, onehot, hid_own, hid_other, rows_out, rows_mid, rows_next, rows_in, part, part_other) = refs[
        at : at + 12
    ]
    local_sem, send_sem, recv_sem, pair_sem, plane_sem, line_sem = refs[at + 12 :]

    f = lax.axis_index("feat")
    me = lax.axis_index("dom")
    z, q = me // plane, me % plane
    barrier = pltpu.get_barrier_semaphore()
    partners = [{"feat": 1 - f}]
    partners += [{"dom": z * plane + (q + d) % plane} for d in range(1, plane)]
    partners += [{"dom": (z + d) % nz * plane + q} for d in range(1, nz)]
    for partner in partners:
        pl.semaphore_signal(barrier, inc=1, device_id=partner, device_id_type=MESH)
    pl.semaphore_wait(barrier, len(partners))

    def message(k, share, piece, src):
        number = sum(p[2] for p in plan[:k]) + piece
        axis, i = steps_of(parts, share)[k]
        return pltpu.make_async_remote_copy(
            src_ref=src,
            dst_ref=receive[k][share].at[piece],
            send_sem=send_sem.at[share, number],
            recv_sem=recv_sem.at[share, number],
            device_id={"dom": partner_of(parts, me, f, axis, i)},
            device_id_type=MESH,
        )

    in_flight = {}
    for piece in range(plan[0][2]):
        for share in range(n_shares):
            copy = message(0, share, piece, messages[share].at[piece])
            copy.start()
            in_flight[0, share, piece] = copy
    loads = []
    for share in range(n_shares):
        copy = pltpu.make_async_copy(keeps[share], work[share], local_sem.at[share])
        copy.start()
        loads.append(copy)

    lanes = lax.broadcasted_iota(jnp.int32, onehot.shape[1:], 1)
    for b in range(onehot.shape[0]):
        ids = list_ref[pl.ds(b * onehot.shape[1], onehot.shape[1]), :]
        onehot[b] = jnp.where(ids == lanes, 1.0, 0.0).astype(jnp.bfloat16)
    for copy in loads:
        copy.wait()

    def absorb(k, share, piece, low, high):
        count, size, pieces, coded = plan[k]
        length = SHARES[share][1]
        first = (pieces - 1 - piece) * size
        if coded:
            decode_add(receive[k][share].at[piece], size, length, low, high, work[share], first, scale)
        else:
            for j in range(low, high):
                work[share][first + j] += receive[k][share][piece, j]

    def forward(k, share, piece):
        count, size, pieces, coded = plan[k]
        first = count + (pieces - 1 - piece) * size
        if coded:
            out = outgoing[k][share].at[piece]
            encode(lambda j: work[share][first + j], size, SHARES[share][1], out, peak, inv)
        else:
            out = work[share].at[pl.ds(first, size)]
        copy = message(k, share, piece, out)
        copy.start()
        in_flight[k, share, piece] = copy

    for k, (count, size, pieces, coded) in enumerate(plan):
        for piece in range(pieces):
            for share in range(n_shares):
                in_flight[k, share, piece].wait_recv()
                if pieces > 1:
                    absorb(k, share, piece, 0, size)
                    if piece < pieces // 2:
                        forward(k + 1, share, piece)
                elif k + 1 < len(plan):
                    absorb(k, share, piece, size // 2, size)
                    forward(k + 1, share, 0)
                    absorb(k, share, piece, 0, size // 2)
                else:
                    absorb(k, share, piece, 0, size)

    for share, (start, length) in enumerate(SHARES):
        total = work[share][0] + own_ref[start : start + length, :]
        work[share][0] = jnp.maximum(total, 0.0)
    hid_own[...] = jnp.concatenate([work[share][0] for share in range(n_shares)], axis=0).astype(jnp.bfloat16)

    def to_pair(src, dst, number):
        return pltpu.make_async_remote_copy(
            src_ref=src,
            dst_ref=dst,
            send_sem=pair_sem.at[0, number],
            recv_sem=pair_sem.at[1, number],
            device_id={"feat": 1 - f},
            device_id_type=MESH,
        )

    share_hidden = to_pair(hid_own, hid_other, 0)
    share_hidden.start()
    share_hidden.wait()
    width = hid_own.shape[1] // 2
    mine, theirs = hid_own[...], hid_other[...]
    own_half = jnp.where(f == 0, mine[:, :width], mine[:, width:])
    other_half = jnp.where(f == 0, theirs[:, :width], theirs[:, width:])
    low = jnp.where(f == 0, own_half, other_half)
    high = jnp.where(f == 0, other_half, own_half)
    hidden = jnp.concatenate([low, high], axis=0)
    per_plane = rows_out.shape[1]
    for b in range(plane):
        rows_out[b] = jnp.dot(onehot[b], hidden, preferred_element_type=jnp.float32).astype(jnp.bfloat16)

    plane_copies = []
    for d in range(1, plane):
        to = (q + d) % plane
        copy = pltpu.make_async_remote_copy(
            src_ref=rows_out.at[to],
            dst_ref=rows_mid.at[q],
            send_sem=plane_sem.at[0, d],
            recv_sem=plane_sem.at[1, d],
            device_id={"dom": z * plane + to},
            device_id_type=MESH,
        )
        copy.start()
        plane_copies.append(copy)
    rows_mid[q] = rows_out[q]
    for copy in plane_copies:
        copy.wait_recv()
    slots = per_plane // nz
    arrived = [rows_mid[s].astype(jnp.float32) for s in range(plane)]
    for r in range(nz):
        rows_next[r] = jnp.concatenate(
            [v[r * slots : (r + 1) * slots, :] for v in arrived], axis=0
        ).astype(jnp.bfloat16)
    line_copies = []
    for d in range(1, nz):
        to = (z + d) % nz
        copy = pltpu.make_async_remote_copy(
            src_ref=rows_next.at[to],
            dst_ref=rows_in.at[z],
            send_sem=line_sem.at[0, d],
            recv_sem=line_sem.at[1, d],
            device_id={"dom": to * plane + q},
            device_id_type=MESH,
        )
        copy.start()
        line_copies.append(copy)
    rows_in[z] = rows_next[z]
    half_rows = pl.ds(pl.multiple_of(f * width, width), width)
    n_own = hidden.shape[0]
    total = jnp.dot(adj_ref[:, :n_own], hidden, preferred_element_type=jnp.float32)
    logits = jnp.dot(hidden[: out_ref.shape[0]], w_self_ref[half_rows, :], preferred_element_type=jnp.float32)
    for copy in line_copies:
        copy.wait_recv()
    pool = jnp.concatenate([rows_in[s] for s in range(nz)], axis=0)
    total += jnp.dot(adj_ref[:, n_own:], pool, preferred_element_type=jnp.float32)
    logits += jnp.dot(total.astype(jnp.bfloat16), w_neigh_ref[half_rows, :], preferred_element_type=jnp.float32)
    part[...] = logits
    share_logits = to_pair(part, part_other, 1)
    share_logits.start()
    share_logits.wait()
    out_ref[...] = part[...] + part_other[...]
    for copy in plane_copies + line_copies:
        copy.wait_send()
    for copy in in_flight.values():
        copy.wait_send()


def second_layer(parts, keeps, messages, own, lists, adj, w_self, w_neigh):
    nx, ny, nz = DIMS[parts]
    plane = nx * ny
    plan = message_plan(parts)
    whole = pl.BlockSpec(memory_space=pltpu.VMEM)
    anywhere = pl.BlockSpec(memory_space=pl.ANY)
    rows, width = own.shape
    half = width // 2
    lengths = [length for _, length in SHARES]
    slots = lists.shape[0] // parts
    buffers = [pltpu.VMEM(a.shape, jnp.float32) for a in keeps]
    for count, size, pieces, coded in plan:
        for n in lengths:
            if coded:
                buffers.append(pltpu.VMEM((pieces, size * n + size, half), jnp.int32))
            else:
                buffers.append(pltpu.VMEM((pieces, size, n, width), jnp.float32))
    for k, (count, size, pieces, coded) in enumerate(plan):
        if coded and k > 0:
            buffers += [pltpu.VMEM((pieces, size * n + size, half), jnp.int32) for n in lengths]
    chunk = max(chunk_of(parts), 8)
    buffers += [pltpu.VMEM((chunk, half), jnp.float32)] * 3
    buffers += [
        pltpu.VMEM((plane, nz * slots, 2 * rows), jnp.bfloat16),
        pltpu.VMEM((rows, width), jnp.bfloat16),
        pltpu.VMEM((rows, width), jnp.bfloat16),
        pltpu.VMEM((plane, nz * slots, half), jnp.bfloat16),
        pltpu.VMEM((plane, nz * slots, half), jnp.bfloat16),
        pltpu.VMEM((nz, plane * slots, half), jnp.bfloat16),
        pltpu.VMEM((nz, plane * slots, half), jnp.bfloat16),
        pltpu.VMEM((adj.shape[0], w_self.shape[1]), jnp.float32),
        pltpu.VMEM((adj.shape[0], w_self.shape[1]), jnp.float32),
    ]
    numbers = sum(p[2] for p in plan)
    dma = pltpu.SemaphoreType.DMA
    buffers += [
        dma((len(SHARES),)),
        dma((len(SHARES), numbers)),
        dma((len(SHARES), numbers)),
        dma((2, 2)),
        dma((2, plane)),
        dma((2, nz)),
    ]
    return pl.pallas_call(
        functools.partial(second_layer_kernel, parts),
        out_shape=jax.ShapeDtypeStruct((adj.shape[0], w_self.shape[1]), jnp.float32),
        in_specs=[anywhere] * 6 + [whole] * 5,
        out_specs=whole,
        scratch_shapes=buffers,
        compiler_params=pltpu.CompilerParams(
            collective_id=1, has_side_effects=True, vmem_limit_bytes=VMEM_LIMIT
        ),
        name="reduce_and_second_layer",
    )(*keeps, *messages, own, lists, adj, w_self, w_neigh)


def body(
    features,
    tile_weight,
    tile_dst,
    tile_src,
    tile_rows,
    w_self1,
    neighbour_weight_first,
    send_list,
    send_count,
    adj_two,
    w_self2,
    w_neigh2,
):
    parts = lax.axis_size("dom")
    f, me = lax.axis_index("feat"), lax.axis_index("dom")
    nx, ny, nz = DIMS[parts]
    slots = send_list.shape[2]
    lists = lax.dynamic_index_in_dim(send_list, me, 0, keepdims=False)
    counts = lax.dynamic_index_in_dim(send_count, me, 0, keepdims=False)
    lists = jnp.where(jnp.arange(slots)[None, :] < counts[:, None], lists, -1)
    lists = lists.reshape(nz, nx * ny, slots).transpose(1, 0, 2).reshape(parts * slots, 1)
    where = jnp.stack([f, me]).astype(jnp.int32)

    other, wn_other, ws_other = swap(features, neighbour_weight_first, w_self1)
    results = first_layer(
        parts,
        where,
        tile_dst,
        tile_src,
        tile_rows,
        features,
        other,
        neighbour_weight_first,
        wn_other,
        w_self1,
        ws_other,
        tile_weight,
    )
    return second_layer(parts, results[:3], results[3:6], results[6], lists, adj_two, w_self2, w_neigh2)


def solution(mesh):
    in_specs = (
        P("dom", "feat"),
        P("dom", None, None),
        P("dom"),
        P("dom"),
        P("dom"),
        P("feat", None),
        P("feat", None),
        P(),
        P(),
        P("dom", None),
        P(),
        P(),
    )
    out_specs = P("dom", None)
    return jax.shard_map(body, mesh=mesh, in_specs=in_specs, out_specs=out_specs, check_vma=False)
```

```python
import functools

import jax
import jax.numpy as jnp
import numpy as np
from jax import lax
from jax.experimental import pallas as pl
from jax.experimental.pallas import tpu as pltpu
from jax.sharding import PartitionSpec as P

DIMS = {128: (4, 4, 8), 16: (4, 2, 2)}
SHARES = ((0, 24), (24, 24), (48, 16))
ORDERS = ((0, 1, 2), (1, 0, 2), (2, 0, 1))
GROUP = 4
GROUPS = 2
VMEM_LIMIT = 56 * 1024 * 1024
MESH = pl.DeviceIdType.MESH


def bits_of(count):
    return count.bit_length() - 1


def steps_of(parts, share):
    dims = DIMS[parts]
    return [(axis, i) for axis in ORDERS[share] for i in range(bits_of(dims[axis]))]


def chunk_of(parts):
    return parts // 8


def packed_from(parts):
    return 8 if parts >= 128 else 2


@functools.lru_cache(maxsize=None)
def slot_table(parts):
    nx, ny, nz = DIMS[parts]
    table = np.zeros((2, len(SHARES), parts), np.int32)
    for f in range(2):
        for share in range(len(SHARES)):
            for b in range(parts):
                coords = (b % nx, b // nx % ny, b // (nx * ny))
                slot = 0
                for axis, i in steps_of(parts, share):
                    n = DIMS[parts][axis]
                    c = (coords[axis] - f) % n
                    slot = slot * 2 + ((c ^ (c >> 1)) >> i & 1)
                table[f, share, b] = slot
    return table


def place_of(parts, me):
    nx, ny, nz = DIMS[parts]
    return lax.rem(me, nx), lax.rem(lax.div(me, nx), ny), lax.div(me, nx * ny)


def partners_of(parts, me, f):
    nx, ny, nz = DIMS[parts]
    place = place_of(parts, me)
    pitch = (1, nx, nx * ny)
    found = {}
    for axis, n in enumerate(DIMS[parts]):
        c = lax.rem(place[axis] - f + n, n)
        for i in range(bits_of(n)):
            size = 2 ** (i + 1)
            at = lax.rem(c, size)
            other = lax.rem(c + (size - 1) - 2 * at + f, n)
            found[axis, i] = me + (other - place[axis]) * pitch[axis]
    return found


def swap_kernel(x_ref, wn_ref, ws_ref, xo_ref, wno_ref, wso_ref, send, recv):
    other = 1 - lax.axis_index("feat")
    barrier = pltpu.get_barrier_semaphore()
    pl.semaphore_signal(barrier, inc=1, device_id={"feat": other}, device_id_type=MESH)
    pl.semaphore_wait(barrier, 1)
    copies = []
    for k, (a, b) in enumerate(((x_ref, xo_ref), (wn_ref, wno_ref), (ws_ref, wso_ref))):
        copy = pltpu.make_async_remote_copy(
            src_ref=a,
            dst_ref=b,
            send_sem=send.at[k],
            recv_sem=recv.at[k],
            device_id={"feat": other},
            device_id_type=MESH,
        )
        copy.start()
        copies.append(copy)
    for copy in copies:
        copy.wait()


def swap(features, wn, ws):
    anywhere = pl.BlockSpec(memory_space=pl.ANY)
    return pl.pallas_call(
        swap_kernel,
        out_shape=[jax.ShapeDtypeStruct(a.shape, a.dtype) for a in (features, wn, ws)],
        in_specs=[anywhere] * 3,
        out_specs=[anywhere] * 3,
        scratch_shapes=[pltpu.SemaphoreType.DMA((3,)), pltpu.SemaphoreType.DMA((3,))],
        compiler_params=pltpu.CompilerParams(collective_id=0, has_side_effects=True),
        name="swap_halves",
    )(features, wn, ws)


def encode(load, count, rows, out, peak, inv):
    def largest(j, carry):
        v = jnp.abs(load(j))
        half = v.shape[1] // 2
        peak[pl.ds(j, 1), :] = jnp.max(jnp.maximum(v[:, :half], v[:, half:]), axis=0, keepdims=True)
        return carry

    lax.fori_loop(0, count, largest, 0, unroll=True)
    top = jnp.maximum(peak[:count, :], 1e-30)
    code = jnp.ceil(jnp.log2(top) * 256.0) + 1.0
    out[count * rows :, :] = code.astype(jnp.int32)
    inv[:count, :] = jnp.exp2(code * (-1.0 / 256.0)) * 32767.0

    def pack(j, carry):
        v = load(j)
        half = v.shape[1] // 2
        s = inv[pl.ds(j, 1), :]
        low = jnp.round(v[:, :half] * s).astype(jnp.int32)
        high = jnp.round(v[:, half:] * s).astype(jnp.int32)
        out[pl.ds(j * rows, rows), :] = jnp.bitwise_or(
            jnp.left_shift(high, 16), jnp.bitwise_and(low, 0xFFFF)
        )
        return carry

    lax.fori_loop(0, count, pack, 0, unroll=True)


def decode_add(src, total, rows, low, high, work, first, scale):
    count = high - low
    code = src[total * rows :, :].astype(jnp.float32)
    scale[:total, :] = jnp.exp2(code * (1.0 / 256.0)) * (1.0 / 32767.0)

    def add(j, carry):
        word = src[pl.ds((low + j) * rows, rows), :]
        s = scale[pl.ds(low + j, 1), :]
        a = jnp.right_shift(jnp.left_shift(word, 16), 16).astype(jnp.float32) * s
        b = jnp.right_shift(word, 16).astype(jnp.float32) * s
        half = a.shape[1]
        work[first + low + j, :, :half] += a
        work[first + low + j, :, half:] += b
        return carry

    lax.fori_loop(0, count, add, 0, unroll=True)


def first_layer_kernel(parts, *refs):
    table, dst, src, limit = refs[:4]
    inputs = refs[4:11]
    keeps, messages, own_out = refs[11:14], refs[14:17], refs[17]
    accs, sends = refs[18:21], refs[21:24]
    held = refs[24:31]
    order, count, plan, gathered, own, peak, inv, sem, load_sem = refs[31:]
    xa, xb, wa, wb, sa, sb, tiles = held
    f, me = lax.axis_index("feat"), lax.axis_index("dom")
    n_tiles, rows, size = tiles.shape
    blocks = xa.shape[0] // size
    half = parts // 2
    depth = xa.shape[1]
    group_rows = GROUP * rows

    loads = []
    for k in range(7):
        source = inputs[k].at[:, pl.ds(pl.multiple_of(f * rows, rows), rows), :] if k == 6 else inputs[k]
        copy = pltpu.make_async_copy(source, held[k], load_sem.at[k])
        copy.start()
        loads.append(copy)

    for s in range(blocks):
        count[s] = 0

    def place(t, carry):
        s = src[t]
        at = count[s]
        order[s, at] = t
        count[s] = at + 1
        return carry

    lax.fori_loop(0, n_tiles, place, 0)

    def groups_of(s, at):
        n = count[s]

        def one(g, at):
            plan[0, at] = s
            plan[1, at] = g * GROUP
            plan[2, at] = jnp.minimum(n - g * GROUP, GROUP)
            return at + 1

        return lax.fori_loop(0, lax.div(n + GROUP - 1, GROUP), one, at)

    n_groups = lax.fori_loop(0, blocks, groups_of, 0)
    for g in range(3 * GROUPS):
        plan[0, n_groups + g] = 0
        plan[1, n_groups + g] = 0
        plan[2, n_groups + g] = 0

    def clear(j, carry):
        for acc in accs:
            acc[j] = jnp.zeros(acc.shape[1:], jnp.float32)
        return carry

    lax.fori_loop(0, parts, clear, 0, unroll=4)
    for copy in loads:
        copy.wait()

    mine = pl.ds(pl.multiple_of(f * rows, rows), rows)
    own[...] = jnp.dot(xa[mine, :], sa[...], preferred_element_type=jnp.float32) + jnp.dot(
        xb[mine, :], sb[...], preferred_element_type=jnp.float32
    )
    own_copy = pltpu.make_async_copy(own, own_out, load_sem.at[7])
    own_copy.start()
    row_ids = lax.broadcasted_iota(jnp.int32, (rows, size), 0) + f * rows
    bases = [table[f, share, me] for share in range(len(SHARES))]

    def gather(g, buffer):
        for u in range(GROUPS):
            s, first, n = plan[0, g + u], plan[1, g + u], plan[2, g + u]
            pieces = []
            for j in range(GROUP):
                valid = j < n
                t = jnp.where(valid, order[s, first + j], 0)
                tile = tiles[t]
                pieces.append(jnp.where(row_ids < jnp.where(valid, limit[t], 0), tile, jnp.zeros_like(tile)))
            a = jnp.concatenate(pieces, axis=0)
            at_source = pl.ds(pl.multiple_of(s * size, size), size)
            at = slice(u * group_rows, (u + 1) * group_rows)
            buffer[at, :depth] = jnp.dot(a, xa[at_source, :], preferred_element_type=jnp.float32).astype(
                jnp.bfloat16
            )
            buffer[at, depth:] = jnp.dot(a, xb[at_source, :], preferred_element_type=jnp.float32).astype(
                jnp.bfloat16
            )

    def spread(g, buffer):
        h = jnp.dot(buffer[:, :depth], wa[...], preferred_element_type=jnp.float32) + jnp.dot(
            buffer[:, depth:], wb[...], preferred_element_type=jnp.float32
        )
        for u in range(GROUPS):
            s, first, n = plan[0, g + u], plan[1, g + u], plan[2, g + u]
            for j in range(GROUP):
                d = dst[jnp.where(j < n, order[s, first + j], 0)]
                for share, (start, length) in enumerate(SHARES):
                    slot = jnp.bitwise_xor(table[f, share, d], bases[share])
                    at = (u * GROUP + j) * rows + start
                    accs[share][slot] += h[at : at + length, :]

    gather(0, gathered.at[0])

    def step(i, carry):
        g = i * (2 * GROUPS)
        spread(g, gathered.at[0])
        gather(g + GROUPS, gathered.at[1])
        spread(g + GROUPS, gathered.at[1])
        gather(g + 2 * GROUPS, gathered.at[0])
        return carry

    lax.fori_loop(0, lax.div(n_groups + 2 * GROUPS - 1, 2 * GROUPS), step, 0)

    copies = [own_copy]
    for share in range(len(SHARES)):
        copy = pltpu.make_async_copy(accs[share].at[pl.ds(0, half)], keeps[share], sem.at[share, 0])
        copy.start()
        copies.append(copy)
    chunk = chunk_of(parts)
    pieces = half // chunk
    for piece in range(pieces):
        for share, (start, length) in enumerate(SHARES):
            acc = accs[share]
            first = half + (pieces - 1 - piece) * chunk
            out = sends[share].at[piece]
            encode(lambda j: acc[first + j], chunk, length, out, peak, inv)
            copy = pltpu.make_async_copy(out, messages[share].at[piece], sem.at[share, 1 + piece])
            copy.start()
            copies.append(copy)
    for copy in copies:
        copy.wait()


def first_layer(parts, dst, src, limit, features, other, wn, wn_other, ws, ws_other, tiles):
    n_tiles, size, _ = tiles.shape
    rows = size // 2
    width = wn.shape[1]
    half = parts // 2
    chunk = chunk_of(parts)
    pieces = half // chunk
    scalars = pl.BlockSpec(memory_space=pltpu.SMEM)
    anywhere = pl.BlockSpec(memory_space=pl.ANY)
    lengths = [length for _, length in SHARES]
    message = [(pieces, chunk * n + chunk, width // 2) for n in lengths]
    operands = (features, other, wn, wn_other, ws, ws_other)
    blocks = features.shape[0] // size
    return pl.pallas_call(
        functools.partial(first_layer_kernel, parts),
        in_specs=[scalars] * 4 + [anywhere] * 7,
        out_specs=[anywhere] * 7,
        scratch_shapes=[pltpu.VMEM((parts, n, width), jnp.float32) for n in lengths]
        + [pltpu.VMEM(shape, jnp.int32) for shape in message]
        + [pltpu.VMEM(a.shape, a.dtype) for a in operands]
        + [
            pltpu.VMEM((n_tiles, rows, size), tiles.dtype),
            pltpu.SMEM((blocks, n_tiles + GROUP), jnp.int32),
            pltpu.SMEM((blocks,), jnp.int32),
            pltpu.SMEM((3, n_tiles // GROUP + blocks + 3 * GROUPS), jnp.int32),
            pltpu.VMEM((2, GROUPS * GROUP * rows, 2 * features.shape[1]), jnp.bfloat16),
            pltpu.VMEM((rows, width), jnp.float32),
            pltpu.VMEM((max(chunk, 8), width // 2), jnp.float32),
            pltpu.VMEM((max(chunk, 8), width // 2), jnp.float32),
            pltpu.SemaphoreType.DMA((len(SHARES), 1 + pieces)),
            pltpu.SemaphoreType.DMA((8,)),
        ],
        out_shape=[jax.ShapeDtypeStruct((half, n, width), jnp.float32) for n in lengths]
        + [jax.ShapeDtypeStruct(shape, jnp.int32) for shape in message]
        + [jax.ShapeDtypeStruct((rows, width), jnp.float32)],
        compiler_params=pltpu.CompilerParams(vmem_limit_bytes=VMEM_LIMIT),
        name="first_layer",
    )(jnp.asarray(slot_table(parts)), dst, src, limit, *operands, tiles)


def message_plan(parts):
    plan = []
    count = parts // 2
    while count >= 1:
        size = min(count, chunk_of(parts))
        plan.append((count, size, count // size, count >= packed_from(parts)))
        count //= 2
    return plan


def second_layer_kernel(parts, *refs):
    nx, ny, nz = DIMS[parts]
    plane = nx * ny
    plan = message_plan(parts)
    n_shares = len(SHARES)
    keeps, messages = refs[0:3], refs[3:6]
    own_ref, list_ref, count_ref, adj_ref, w_self_ref, w_neigh_ref, out_ref = refs[6:13]
    at = 13
    work = refs[at : at + 3]
    at += 3
    receive, outgoing = [], []
    for k in range(len(plan)):
        receive.append(refs[at : at + 3])
        at += 3
    for k in range(len(plan)):
        coded = plan[k][3] and k > 0
        outgoing.append(refs[at : at + 3] if coded else None)
        at += 3 if coded else 0
    (peak, inv, scale, lists, onehot, hid_own, hid_other, rows_out, rows_in, part, part_other) = refs[at : at + 11]
    local_sem, send_sem, recv_sem, pair_sem, rows_sem = refs[at + 11 :]

    f = lax.axis_index("feat")
    me = lax.axis_index("dom")
    partners = partners_of(parts, me, f)
    rows_in[...] = jnp.zeros_like(rows_in)
    barrier = pltpu.get_barrier_semaphore()
    for target in [{"feat": 1 - f}] + [{"dom": dom} for dom in partners.values()]:
        pl.semaphore_signal(barrier, inc=1, device_id=target, device_id_type=MESH)
    pl.semaphore_wait(barrier, 1 + len(partners))

    def message(k, share, piece, src):
        number = sum(p[2] for p in plan[:k]) + piece
        return pltpu.make_async_remote_copy(
            src_ref=src,
            dst_ref=receive[k][share].at[piece],
            send_sem=send_sem.at[share, number],
            recv_sem=recv_sem.at[share, number],
            device_id={"dom": partners[steps_of(parts, share)[k]]},
            device_id_type=MESH,
        )

    in_flight = {}
    for piece in range(plan[0][2]):
        for share in range(n_shares):
            copy = message(0, share, piece, messages[share].at[piece])
            copy.start()
            in_flight[0, share, piece] = copy
    loads = []
    for share in range(n_shares):
        copy = pltpu.make_async_copy(keeps[share], work[share], local_sem.at[share])
        copy.start()
        loads.append(copy)

    get_lists = pltpu.make_async_copy(list_ref.at[me], lists, local_sem.at[len(SHARES)])
    get_lists.start()
    get_lists.wait()
    slots = lists.shape[0]
    shape = lists.shape
    lanes = lax.broadcasted_iota(jnp.int32, shape, 1)
    valid = lax.broadcasted_iota(jnp.int32, shape, 0) < count_ref[pl.ds(me, 1), :]
    wanted = jnp.where(valid, lists[...], -1).astype(jnp.float32)
    hidden_rows = onehot.shape[1]
    ids = lax.broadcasted_iota(jnp.int32, (slots, hidden_rows), 1).astype(jnp.float32)
    px, py, pz = place_of(parts, me)
    at_x = [lax.rem(px + d, nx) for d in range(nx)]
    at_y = [lax.rem(py + d, ny) * nx for d in range(ny)]
    at_z = [lax.rem(pz + d, nz) * (nx * ny) for d in range(nz)]
    receivers = []
    for d in range(nz // 2):
        by_parity = [jnp.where(f == odd, at_z[2 * d], at_z[2 * d + 1]) for odd in range(2)]
        for dy in range(ny):
            for dx in range(nx):
                receivers.append(at_x[dx] + at_y[dy] + by_parity[(dx + dy) % 2])

    for i in range(0, len(receivers), 2):
        pair = []
        for r in receivers[i : i + 2]:
            column = jnp.sum(jnp.where(lanes == r, wanted, 0.0), axis=1, keepdims=True)
            pair.append(jnp.where(column == ids, 1.0, 0.0))
        onehot[i * slots : (i + 2) * slots, :] = jnp.concatenate(pair, axis=0).astype(jnp.bfloat16)
    for copy in loads:
        copy.wait()

    def absorb(k, share, piece, low, high):
        count, size, pieces, coded = plan[k]
        length = SHARES[share][1]
        first = (pieces - 1 - piece) * size
        if coded:
            decode_add(receive[k][share].at[piece], size, length, low, high, work[share], first, scale)
        else:
            for j in range(low, high):
                work[share][first + j] += receive[k][share][piece, j]

    def forward(k, share, piece):
        count, size, pieces, coded = plan[k]
        first = count + (pieces - 1 - piece) * size
        if coded:
            out = outgoing[k][share].at[piece]
            encode(lambda j: work[share][first + j], size, SHARES[share][1], out, peak, inv)
        else:
            out = work[share].at[pl.ds(first, size)]
        copy = message(k, share, piece, out)
        copy.start()
        in_flight[k, share, piece] = copy

    for k, (count, size, pieces, coded) in enumerate(plan):
        for piece in range(pieces):
            for share in range(n_shares):
                in_flight[k, share, piece].wait_recv()
                if pieces > 1:
                    absorb(k, share, piece, 0, size)
                    if piece < pieces // 2:
                        forward(k + 1, share, piece)
                elif k + 1 < len(plan):
                    absorb(k, share, piece, size // 2, size)
                    forward(k + 1, share, 0)
                    absorb(k, share, piece, 0, size // 2)
                else:
                    absorb(k, share, piece, 0, size)

    for share, (start, length) in enumerate(SHARES):
        total = work[share][0] + own_ref[start : start + length, :]
        work[share][0] = jnp.maximum(total, 0.0)
    hid_own[...] = jnp.concatenate([work[share][0] for share in range(n_shares)], axis=0).astype(jnp.bfloat16)

    def to_pair(src, dst, number):
        return pltpu.make_async_remote_copy(
            src_ref=src,
            dst_ref=dst,
            send_sem=pair_sem.at[0, number],
            recv_sem=pair_sem.at[1, number],
            device_id={"feat": 1 - f},
            device_id_type=MESH,
        )

    share_hidden = to_pair(hid_own, hid_other, 0)
    share_hidden.start()
    share_hidden.wait()
    mine, theirs = hid_own[...], hid_other[...]
    hidden = jnp.concatenate([jnp.where(f == 0, mine, theirs), jnp.where(f == 0, theirs, mine)], axis=0)
    width = hidden.shape[1] // 2
    picked = jnp.dot(onehot[...], hidden, preferred_element_type=jnp.float32)
    for i in range(len(receivers)):
        block = picked[i * slots : (i + 1) * slots, :]
        rows_out[i] = jnp.concatenate([block[:, :width], block[:, width:]], axis=0).astype(jnp.bfloat16)

    def to_receiver(i):
        return pltpu.make_async_remote_copy(
            src_ref=rows_out.at[i],
            dst_ref=rows_in.at[me],
            send_sem=rows_sem.at[0],
            recv_sem=rows_sem.at[1],
            device_id={"dom": receivers[i]},
            device_id_type=MESH,
        )

    for i in range(1, len(receivers)):
        to_receiver(i).start()

    @pl.when(f == 0)
    def _():
        rows_in[me] = rows_out[0]

    @pl.when(f == 1)
    def _():
        to_receiver(0).start()

    n_own = hidden.shape[0]
    out_rows = out_ref.shape[0]
    own_total = jnp.dot(adj_ref[:, :n_own], hidden, preferred_element_type=jnp.float32)
    self_logits = lax.dot_general(
        hidden[:out_rows], w_self_ref[...], (((1,), (1,)), ((), ())), preferred_element_type=jnp.float32
    )
    blocks = len(receivers)

    def wait_rows(n):
        for number, ref in ((0, rows_out), (1, rows_in)):
            pltpu.make_async_copy(ref.at[pl.ds(0, n)], ref.at[pl.ds(0, n)], rows_sem.at[number]).wait()

    pl.when(f == 0)(lambda: wait_rows(blocks - 1))
    pl.when(f == 1)(lambda: wait_rows(blocks))

    arrived = rows_in[...].astype(jnp.float32)
    pool = [
        arrived[:, k * slots : (k + 1) * slots, :].reshape(parts * slots, width).astype(jnp.bfloat16)
        for k in range(2)
    ]
    for k in range(2):
        part[:, k * width : (k + 1) * width] = jnp.dot(
            adj_ref[:, n_own:], pool[k], preferred_element_type=jnp.float32
        )
    share_part = to_pair(part, part_other, 1)
    share_part.start()
    share_part.wait()
    aggregate = (part[...] + part_other[...] + own_total).astype(jnp.bfloat16)
    out_ref[...] = self_logits + lax.dot_general(
        aggregate, w_neigh_ref[...], (((1,), (1,)), ((), ())), preferred_element_type=jnp.float32
    )
    for copy in in_flight.values():
        copy.wait_send()


def second_layer(parts, keeps, messages, own, lists, counts, adj, w_self, w_neigh):
    plan = message_plan(parts)
    whole = pl.BlockSpec(memory_space=pltpu.VMEM)
    anywhere = pl.BlockSpec(memory_space=pl.ANY)
    rows, width = own.shape
    half = width // 2
    lengths = [length for _, length in SHARES]
    slots = lists.shape[1]
    buffers = [pltpu.VMEM(a.shape, jnp.float32) for a in keeps]
    for count, size, pieces, coded in plan:
        for n in lengths:
            if coded:
                buffers.append(pltpu.VMEM((pieces, size * n + size, half), jnp.int32))
            else:
                buffers.append(pltpu.VMEM((pieces, size, n, width), jnp.float32))
    for k, (count, size, pieces, coded) in enumerate(plan):
        if coded and k > 0:
            buffers += [pltpu.VMEM((pieces, size * n + size, half), jnp.int32) for n in lengths]
    chunk = max(chunk_of(parts), 8)
    buffers += [pltpu.VMEM((chunk, half), jnp.float32)] * 3
    buffers += [
        pltpu.VMEM(lists.shape[1:], jnp.int32),
        pltpu.VMEM((parts // 2 * slots, 2 * rows), jnp.bfloat16),
        pltpu.VMEM((rows, width), jnp.bfloat16),
        pltpu.VMEM((rows, width), jnp.bfloat16),
        pltpu.VMEM((parts // 2, 2 * slots, half), jnp.bfloat16),
        pltpu.VMEM((parts, 2 * slots, half), jnp.bfloat16),
        pltpu.VMEM((adj.shape[0], width), jnp.float32),
        pltpu.VMEM((adj.shape[0], width), jnp.float32),
    ]
    numbers = sum(p[2] for p in plan)
    dma = pltpu.SemaphoreType.DMA
    buffers += [
        dma((len(SHARES) + 1,)),
        dma((len(SHARES), numbers)),
        dma((len(SHARES), numbers)),
        dma((2, 2)),
        dma((2,)),
    ]
    return pl.pallas_call(
        functools.partial(second_layer_kernel, parts),
        out_shape=jax.ShapeDtypeStruct((adj.shape[0], w_self.shape[0]), jnp.float32),
        in_specs=[anywhere] * 6 + [whole, anywhere] + [whole] * 4,
        out_specs=whole,
        scratch_shapes=buffers,
        compiler_params=pltpu.CompilerParams(
            collective_id=1, has_side_effects=True, vmem_limit_bytes=VMEM_LIMIT
        ),
        name="reduce_and_second_layer",
    )(*keeps, *messages, own, lists, counts, adj, w_self, w_neigh)


def body(
    features,
    tile_weight,
    tile_dst,
    tile_src,
    tile_rows,
    w_self1,
    neighbour_weight_first,
    send_list,
    send_count,
    adj_two,
    w_self2,
    w_neigh2,
):
    parts = lax.axis_size("dom")
    other, wn_other, ws_other = swap(features, neighbour_weight_first, w_self1)
    results = first_layer(
        parts,
        tile_dst,
        tile_src,
        tile_rows,
        features,
        other,
        neighbour_weight_first,
        wn_other,
        w_self1,
        ws_other,
        tile_weight,
    )
    return second_layer(parts, results[:3], results[3:6], results[6], send_list.transpose(0, 2, 1), send_count, adj_two, w_self2.T, w_neigh2.T)


def solution(mesh):
    in_specs = (
        P("dom", "feat"),
        P("dom", None, None),
        P("dom"),
        P("dom"),
        P("dom"),
        P("feat", None),
        P("feat", None),
        P(),
        P(),
        P("dom", None),
        P(),
        P(),
    )
    out_specs = P("dom", None)
    return jax.shard_map(body, mesh=mesh, in_specs=in_specs, out_specs=out_specs, check_vma=False)
```

```python
import functools

import jax
import jax.numpy as jnp
import numpy as np
from jax import lax
from jax.experimental import pallas as pl
from jax.experimental.pallas import tpu as pltpu
from jax.sharding import PartitionSpec as P

DIMS = {128: (4, 4, 8), 16: (4, 2, 2)}
SHARES = ((0, 24), (24, 24), (48, 16))


def stages_of(parts, share):
    bits = [[(axis, i) for i in range(bits_of(n))] for axis, n in enumerate(DIMS[parts])]
    x, y, z = bits
    if share == 0:
        return [x[:1], x[1:], y, z]
    if share == 1:
        return [y[:1], y[1:], x, z] if len(y) > 1 else [y, x[:1], x[1:], z]
    return [z[:1], z[1:2], z[2:] + x, y] if len(z) > 1 else [z, x[:1], x[1:], y]


GROUP = 4
GROUPS = 2
VMEM_LIMIT = 56 * 1024 * 1024
MESH = pl.DeviceIdType.MESH


def bits_of(count):
    return count.bit_length() - 1


def steps_of(parts, share):
    return [bit for stage in stages_of(parts, share) for bit in stage]


def chunk_of(parts):
    return parts // 8


def plan_of(parts, share):
    plan = []
    count = parts
    for bits in stages_of(parts, share):
        stay = count >> len(bits)
        size = min(stay, chunk_of(parts))
        plan.append((bits, stay, stay // size, size))
        count = stay
    return plan


@functools.lru_cache(maxsize=None)
def slot_table(parts):
    nx, ny, nz = DIMS[parts]
    table = np.zeros((2, len(SHARES), parts), np.int32)
    for f in range(2):
        for share in range(len(SHARES)):
            for b in range(parts):
                coords = (b % nx, b // nx % ny, b // (nx * ny))
                slot = 0
                for axis, i in steps_of(parts, share):
                    n = DIMS[parts][axis]
                    c = (coords[axis] - f) % n
                    slot = slot * 2 + ((c ^ (c >> 1)) >> i & 1)
                table[f, share, b] = slot
    return table


def place_of(parts, me):
    nx, ny, nz = DIMS[parts]
    return lax.rem(me, nx), lax.rem(lax.div(me, nx), ny), lax.div(me, nx * ny)


def chip_across(parts, me, f, bits):
    nx, ny, nz = DIMS[parts]
    place = place_of(parts, me)
    pitch = (1, nx, nx * ny)
    dom = me
    for axis, n in enumerate(DIMS[parts]):
        flips = sorted(i for a, i in bits if a == axis)
        if not flips:
            continue
        c = lax.rem(place[axis] - f + n, n)
        for i in flips:
            size = 2 ** (i + 1)
            c = c + (size - 1) - 2 * lax.rem(c, size)
        dom = dom + (lax.rem(c + f, n) - place[axis]) * pitch[axis]
    return dom


def swap_kernel(x_ref, wn_ref, ws_ref, xo_ref, wno_ref, wso_ref, send, recv):
    other = 1 - lax.axis_index("feat")
    barrier = pltpu.get_barrier_semaphore()
    pl.semaphore_signal(barrier, inc=1, device_id={"feat": other}, device_id_type=MESH)
    pl.semaphore_wait(barrier, 1)
    copies = []
    for k, (a, b) in enumerate(((x_ref, xo_ref), (wn_ref, wno_ref), (ws_ref, wso_ref))):
        copy = pltpu.make_async_remote_copy(
            src_ref=a,
            dst_ref=b,
            send_sem=send.at[k],
            recv_sem=recv.at[k],
            device_id={"feat": other},
            device_id_type=MESH,
        )
        copy.start()
        copies.append(copy)
    for copy in copies:
        copy.wait()


def swap(features, wn, ws):
    anywhere = pl.BlockSpec(memory_space=pl.ANY)
    return pl.pallas_call(
        swap_kernel,
        out_shape=[jax.ShapeDtypeStruct(a.shape, a.dtype) for a in (features, wn, ws)],
        in_specs=[anywhere] * 3,
        out_specs=[anywhere] * 3,
        scratch_shapes=[pltpu.SemaphoreType.DMA((3,)), pltpu.SemaphoreType.DMA((3,))],
        compiler_params=pltpu.CompilerParams(collective_id=0, has_side_effects=True),
        name="swap_halves",
    )(features, wn, ws)


def encode(load, count, rows, out, peak, inv):
    def largest(j, carry):
        v = jnp.abs(load(j))
        half = v.shape[1] // 2
        peak[pl.ds(j, 1), :] = jnp.max(jnp.maximum(v[:, :half], v[:, half:]), axis=0, keepdims=True)
        return carry

    lax.fori_loop(0, count, largest, 0, unroll=True)
    top = jnp.maximum(peak[:count, :], 1e-30)
    code = jnp.ceil(jnp.log2(top) * 256.0) + 1.0
    out[count * rows : count * rows + count, :] = code.astype(jnp.int32)
    inv[:count, :] = jnp.exp2(code * (-1.0 / 256.0)) * 32767.0

    def pack(j, carry):
        v = load(j)
        half = v.shape[1] // 2
        s = inv[pl.ds(j, 1), :]
        low = jnp.round(v[:, :half] * s).astype(jnp.int32)
        high = jnp.round(v[:, half:] * s).astype(jnp.int32)
        out[pl.ds(j * rows, rows), :] = jnp.bitwise_or(
            jnp.left_shift(high, 16), jnp.bitwise_and(low, 0xFFFF)
        )
        return carry

    lax.fori_loop(0, count, pack, 0, unroll=True)


def decode_add(src, total, rows, low, high, work, first, scale):
    count = high - low
    code = src[total * rows : total * rows + total, :].astype(jnp.float32)
    scale[:total, :] = jnp.exp2(code * (1.0 / 256.0)) * (1.0 / 32767.0)

    def add(j, carry):
        word = src[pl.ds((low + j) * rows, rows), :]
        s = scale[pl.ds(low + j, 1), :]
        a = jnp.right_shift(jnp.left_shift(word, 16), 16).astype(jnp.float32) * s
        b = jnp.right_shift(word, 16).astype(jnp.float32) * s
        half = a.shape[1]
        work[first + low + j, :, :half] += a
        work[first + low + j, :, half:] += b
        return carry

    lax.fori_loop(0, count, add, 0, unroll=True)


def first_layer_kernel(parts, *refs):
    table, dst, src, limit = refs[:4]
    inputs = refs[4:11]
    keeps, messages, own_out = refs[11:14], refs[14:17], refs[17]
    accs, sends = refs[18:21], refs[21:24]
    held = refs[24:31]
    order, count, plan, gathered, own, peak, inv, sem, load_sem = refs[31:]
    xa, xb, wa, wb, sa, sb, tiles = held
    f, me = lax.axis_index("feat"), lax.axis_index("dom")
    n_tiles, rows, size = tiles.shape
    blocks = xa.shape[0] // size
    half = parts // 2
    depth = xa.shape[1]
    group_rows = GROUP * rows

    loads = []
    for k in range(7):
        source = inputs[k].at[:, pl.ds(pl.multiple_of(f * rows, rows), rows), :] if k == 6 else inputs[k]
        copy = pltpu.make_async_copy(source, held[k], load_sem.at[k])
        copy.start()
        loads.append(copy)

    for s in range(blocks):
        count[s] = 0

    def place(t, carry):
        s = src[t]
        at = count[s]
        order[s, at] = t
        count[s] = at + 1
        return carry

    lax.fori_loop(0, n_tiles, place, 0)

    def groups_of(s, at):
        n = count[s]

        def one(g, at):
            plan[0, at] = s
            plan[1, at] = g * GROUP
            plan[2, at] = jnp.minimum(n - g * GROUP, GROUP)
            return at + 1

        return lax.fori_loop(0, lax.div(n + GROUP - 1, GROUP), one, at)

    n_groups = lax.fori_loop(0, blocks, groups_of, 0)
    for g in range(3 * GROUPS):
        plan[0, n_groups + g] = 0
        plan[1, n_groups + g] = 0
        plan[2, n_groups + g] = 0

    def clear(j, carry):
        for acc in accs:
            acc[j] = jnp.zeros(acc.shape[1:], jnp.float32)
        return carry

    lax.fori_loop(0, parts, clear, 0, unroll=4)
    for copy in loads:
        copy.wait()

    mine = pl.ds(pl.multiple_of(f * rows, rows), rows)
    own[...] = jnp.dot(xa[mine, :], sa[...], preferred_element_type=jnp.float32) + jnp.dot(
        xb[mine, :], sb[...], preferred_element_type=jnp.float32
    )
    own_copy = pltpu.make_async_copy(own, own_out, load_sem.at[7])
    own_copy.start()
    row_ids = lax.broadcasted_iota(jnp.int32, (rows, size), 0) + f * rows
    bases = [table[f, share, me] for share in range(len(SHARES))]

    def gather(g, buffer):
        for u in range(GROUPS):
            s, first, n = plan[0, g + u], plan[1, g + u], plan[2, g + u]
            pieces = []
            for j in range(GROUP):
                valid = j < n
                t = jnp.where(valid, order[s, first + j], 0)
                tile = tiles[t]
                pieces.append(jnp.where(row_ids < jnp.where(valid, limit[t], 0), tile, jnp.zeros_like(tile)))
            a = jnp.concatenate(pieces, axis=0)
            at_source = pl.ds(pl.multiple_of(s * size, size), size)
            at = slice(u * group_rows, (u + 1) * group_rows)
            buffer[at, :depth] = jnp.dot(a, xa[at_source, :], preferred_element_type=jnp.float32).astype(
                jnp.bfloat16
            )
            buffer[at, depth:] = jnp.dot(a, xb[at_source, :], preferred_element_type=jnp.float32).astype(
                jnp.bfloat16
            )

    def spread(g, buffer):
        h = jnp.dot(buffer[:, :depth], wa[...], preferred_element_type=jnp.float32) + jnp.dot(
            buffer[:, depth:], wb[...], preferred_element_type=jnp.float32
        )
        for u in range(GROUPS):
            s, first, n = plan[0, g + u], plan[1, g + u], plan[2, g + u]
            for j in range(GROUP):
                d = dst[jnp.where(j < n, order[s, first + j], 0)]
                for share, (start, length) in enumerate(SHARES):
                    slot = jnp.bitwise_xor(table[f, share, d], bases[share])
                    at = (u * GROUP + j) * rows + start
                    accs[share][slot] += h[at : at + length, :]

    gather(0, gathered.at[0])

    def step(i, carry):
        g = i * (2 * GROUPS)
        spread(g, gathered.at[0])
        gather(g + GROUPS, gathered.at[1])
        spread(g + GROUPS, gathered.at[1])
        gather(g + 2 * GROUPS, gathered.at[0])
        return carry

    lax.fori_loop(0, lax.div(n_groups + 2 * GROUPS - 1, 2 * GROUPS), step, 0)

    copies = [own_copy]
    for share in range(len(SHARES)):
        copy = pltpu.make_async_copy(accs[share].at[pl.ds(0, half)], keeps[share], sem.at[share, 0])
        copy.start()
        copies.append(copy)
    chunk = chunk_of(parts)
    pieces = half // chunk
    for piece in range(pieces):
        for share, (start, length) in enumerate(SHARES):
            acc = accs[share]
            first = half + (pieces - 1 - piece) * chunk
            out = sends[share].at[piece]
            encode(lambda j: acc[first + j], chunk, length, out, peak, inv)
            copy = pltpu.make_async_copy(out, messages[share].at[piece], sem.at[share, 1 + piece])
            copy.start()
            copies.append(copy)
    for copy in copies:
        copy.wait()


def first_layer(parts, dst, src, limit, features, other, wn, wn_other, ws, ws_other, tiles):
    n_tiles, size, _ = tiles.shape
    rows = size // 2
    width = wn.shape[1]
    half = parts // 2
    chunk = chunk_of(parts)
    pieces = half // chunk
    scalars = pl.BlockSpec(memory_space=pltpu.SMEM)
    anywhere = pl.BlockSpec(memory_space=pl.ANY)
    lengths = [length for _, length in SHARES]
    message = [(pieces, chunk * n + chunk, width // 2) for n in lengths]
    operands = (features, other, wn, wn_other, ws, ws_other)
    blocks = features.shape[0] // size
    return pl.pallas_call(
        functools.partial(first_layer_kernel, parts),
        in_specs=[scalars] * 4 + [anywhere] * 7,
        out_specs=[anywhere] * 7,
        scratch_shapes=[pltpu.VMEM((parts, n, width), jnp.float32) for n in lengths]
        + [pltpu.VMEM(shape, jnp.int32) for shape in message]
        + [pltpu.VMEM(a.shape, a.dtype) for a in operands]
        + [
            pltpu.VMEM((n_tiles, rows, size), tiles.dtype),
            pltpu.SMEM((blocks, n_tiles + GROUP), jnp.int32),
            pltpu.SMEM((blocks,), jnp.int32),
            pltpu.SMEM((3, n_tiles // GROUP + blocks + 3 * GROUPS), jnp.int32),
            pltpu.VMEM((2, GROUPS * GROUP * rows, 2 * features.shape[1]), jnp.bfloat16),
            pltpu.VMEM((rows, width), jnp.float32),
            pltpu.VMEM((max(chunk, 8), width // 2), jnp.float32),
            pltpu.VMEM((max(chunk, 8), width // 2), jnp.float32),
            pltpu.SemaphoreType.DMA((len(SHARES), 1 + pieces)),
            pltpu.SemaphoreType.DMA((8,)),
        ],
        out_shape=[jax.ShapeDtypeStruct((half, n, width), jnp.float32) for n in lengths]
        + [jax.ShapeDtypeStruct(shape, jnp.int32) for shape in message]
        + [jax.ShapeDtypeStruct((rows, width), jnp.float32)],
        compiler_params=pltpu.CompilerParams(vmem_limit_bytes=VMEM_LIMIT),
        name="first_layer",
    )(jnp.asarray(slot_table(parts)), dst, src, limit, *operands, tiles)


def second_layer_kernel(parts, *refs):
    nx, ny, nz = DIMS[parts]
    plane = nx * ny
    n_shares = len(SHARES)
    plans = [plan_of(parts, share) for share in range(n_shares)]
    n_stages = len(plans[0])
    keeps, messages = refs[0:3], refs[3:6]
    own_ref, list_ref, count_ref, adj_ref, w_self_ref, w_neigh_ref, out_ref = refs[6:13]
    at = 13
    work = refs[at : at + 3]
    at += 3
    receive, outgoing = [], []
    for k in range(n_stages):
        receive.append(refs[at : at + 3])
        at += 3
    for k in range(n_stages):
        outgoing.append(refs[at : at + 3] if k > 0 else None)
        at += 3 if k > 0 else 0
    (peak, inv, scale, lists, onehot, hid_own, hid_other, rows_out, rows_in, part, part_other) = refs[at : at + 11]
    local_sem, send_sem, recv_sem, pair_sem, rows_sem = refs[at + 11 :]

    f = lax.axis_index("feat")
    me = lax.axis_index("dom")
    partners = {}
    for share in range(n_shares):
        for k, (bits, stay, pieces, size) in enumerate(plans[share]):
            for mask in range(1, 2 ** len(bits)):
                chosen = tuple(sorted(b for i, b in enumerate(bits) if mask >> (len(bits) - 1 - i) & 1))
                if chosen not in partners:
                    partners[chosen] = chip_across(parts, me, f, chosen)
    rows_in[...] = jnp.zeros_like(rows_in)
    barrier = pltpu.get_barrier_semaphore()
    for target in [{"feat": 1 - f}] + [{"dom": dom} for dom in partners.values()]:
        pl.semaphore_signal(barrier, inc=1, device_id=target, device_id_type=MESH)
    pl.semaphore_wait(barrier, 1 + len(partners))

    def message(k, share, mask, piece, src):
        bits, stay, pieces, size = plans[share][k]
        index = (mask - 1) * pieces + piece
        number = sum((2 ** len(p[0]) - 1) * p[2] for p in plans[share][:k]) + index
        chosen = tuple(sorted(b for i, b in enumerate(bits) if mask >> (len(bits) - 1 - i) & 1))
        return pltpu.make_async_remote_copy(
            src_ref=src,
            dst_ref=receive[k][share].at[index],
            send_sem=send_sem.at[share, number],
            recv_sem=recv_sem.at[share, number],
            device_id={"dom": partners[chosen]},
            device_id_type=MESH,
        )

    in_flight = {}
    for piece in range(plans[0][0][2]):
        for share in range(n_shares):
            copy = message(0, share, 1, piece, messages[share].at[piece])
            copy.start()
            in_flight[0, share, 1, piece] = copy
    loads = []
    for share in range(n_shares):
        copy = pltpu.make_async_copy(keeps[share], work[share], local_sem.at[share])
        copy.start()
        loads.append(copy)

    get_lists = pltpu.make_async_copy(list_ref.at[me], lists, local_sem.at[len(SHARES)])
    get_lists.start()
    get_lists.wait()
    slots = lists.shape[0]
    shape = lists.shape
    lanes = lax.broadcasted_iota(jnp.int32, shape, 1)
    valid = lax.broadcasted_iota(jnp.int32, shape, 0) < count_ref[pl.ds(me, 1), :]
    wanted = jnp.where(valid, lists[...], -1).astype(jnp.float32)
    hidden_rows = onehot.shape[1]
    ids = lax.broadcasted_iota(jnp.int32, (slots, hidden_rows), 1).astype(jnp.float32)
    px, py, pz = place_of(parts, me)
    at_x = [lax.rem(px + d, nx) for d in range(nx)]
    at_y = [lax.rem(py + d, ny) * nx for d in range(ny)]
    at_z = [lax.rem(pz + d, nz) * (nx * ny) for d in range(nz)]
    receivers = []
    for d in range(nz // 2):
        by_parity = [jnp.where(f == odd, at_z[2 * d], at_z[2 * d + 1]) for odd in range(2)]
        for dy in range(ny):
            for dx in range(nx):
                receivers.append(at_x[dx] + at_y[dy] + by_parity[(dx + dy) % 2])

    for i in range(0, len(receivers), 2):
        pair = []
        for r in receivers[i : i + 2]:
            column = jnp.sum(jnp.where(lanes == r, wanted, 0.0), axis=1, keepdims=True)
            pair.append(jnp.where(column == ids, 1.0, 0.0))
        onehot[i * slots : (i + 2) * slots, :] = jnp.concatenate(pair, axis=0).astype(jnp.bfloat16)
    for copy in loads:
        copy.wait()

    def absorb(k, share, mask, piece, low, high):
        bits, stay, pieces, size = plans[share][k]
        first = (pieces - 1 - piece) * size
        source = receive[k][share].at[(mask - 1) * pieces + piece]
        decode_add(source, size, SHARES[share][1], low - first, high - first, work[share], first, scale)

    def forward(k, share, mask, piece):
        bits, stay, pieces, size = plans[share][k]
        first = mask * stay + (pieces - 1 - piece) * size
        out = outgoing[k][share].at[(mask - 1) * pieces + piece]
        encode(lambda j: work[share][first + j], size, SHARES[share][1], out, peak, inv)
        copy = message(k, share, mask, piece, out)
        copy.start()
        in_flight[k, share, mask, piece] = copy

    for k in range(n_stages):
        for piece in range(plans[0][k][2]):
            for share in reversed(range(n_shares)):
                bits, stay, pieces, size = plans[share][k]
                masks = range(1, 2 ** len(bits))
                for mask in masks:
                    in_flight[k, share, mask, piece].wait_recv()
                top = (pieces - piece) * size
                bottom = top - size
                leaving = []
                if k + 1 < n_stages:
                    next_bits, next_stay, next_pieces, next_size = plans[share][k + 1]
                    for mask in reversed(range(1, 2 ** len(next_bits))):
                        for next_piece in range(next_pieces):
                            low = mask * next_stay + (next_pieces - 1 - next_piece) * next_size
                            if bottom <= low < top:
                                leaving.append((low, low + next_size, mask, next_piece))
                for low, high, mask, next_piece in leaving:
                    for m in masks:
                        absorb(k, share, m, piece, low, high)
                    forward(k + 1, share, mask, next_piece)
                rest = min([low for low, *_ in leaving] + [top])
                if rest > bottom:
                    for m in masks:
                        absorb(k, share, m, piece, bottom, rest)

    for share, (start, length) in enumerate(SHARES):
        total = work[share][0] + own_ref[start : start + length, :]
        work[share][0] = jnp.maximum(total, 0.0)
    hid_own[...] = jnp.concatenate([work[share][0] for share in range(n_shares)], axis=0).astype(jnp.bfloat16)

    def to_pair(src, dst, number):
        return pltpu.make_async_remote_copy(
            src_ref=src,
            dst_ref=dst,
            send_sem=pair_sem.at[0, number],
            recv_sem=pair_sem.at[1, number],
            device_id={"feat": 1 - f},
            device_id_type=MESH,
        )

    share_hidden = to_pair(hid_own, hid_other, 0)
    share_hidden.start()
    share_hidden.wait()
    mine, theirs = hid_own[...], hid_other[...]
    hidden = jnp.concatenate([jnp.where(f == 0, mine, theirs), jnp.where(f == 0, theirs, mine)], axis=0)
    width = hidden.shape[1] // 2
    picked = jnp.dot(onehot[...], hidden, preferred_element_type=jnp.float32)
    for i in range(len(receivers)):
        block = picked[i * slots : (i + 1) * slots, :]
        rows_out[i] = jnp.concatenate([block[:, :width], block[:, width:]], axis=0).astype(jnp.bfloat16)

    def to_receiver(i):
        return pltpu.make_async_remote_copy(
            src_ref=rows_out.at[i],
            dst_ref=rows_in.at[me],
            send_sem=rows_sem.at[0],
            recv_sem=rows_sem.at[1],
            device_id={"dom": receivers[i]},
            device_id_type=MESH,
        )

    for i in range(1, len(receivers)):
        to_receiver(i).start()

    @pl.when(f == 0)
    def _():
        rows_in[me] = rows_out[0]

    @pl.when(f == 1)
    def _():
        to_receiver(0).start()

    n_own = hidden.shape[0]
    out_rows = out_ref.shape[0]
    own_total = jnp.dot(adj_ref[:, :n_own], hidden, preferred_element_type=jnp.float32)
    self_logits = lax.dot_general(
        hidden[:out_rows], w_self_ref[...], (((1,), (1,)), ((), ())), preferred_element_type=jnp.float32
    )
    blocks = len(receivers)

    def wait_rows(n):
        for number, ref in ((0, rows_out), (1, rows_in)):
            pltpu.make_async_copy(ref.at[pl.ds(0, n)], ref.at[pl.ds(0, n)], rows_sem.at[number]).wait()

    pl.when(f == 0)(lambda: wait_rows(blocks - 1))
    pl.when(f == 1)(lambda: wait_rows(blocks))

    arrived = rows_in[...].astype(jnp.float32)
    pool = [
        arrived[:, k * slots : (k + 1) * slots, :].reshape(parts * slots, width).astype(jnp.bfloat16)
        for k in range(2)
    ]
    for k in range(2):
        part[:, k * width : (k + 1) * width] = jnp.dot(
            adj_ref[:, n_own:], pool[k], preferred_element_type=jnp.float32
        )
    share_part = to_pair(part, part_other, 1)
    share_part.start()
    share_part.wait()
    aggregate = (part[...] + part_other[...] + own_total).astype(jnp.bfloat16)
    out_ref[...] = self_logits + lax.dot_general(
        aggregate, w_neigh_ref[...], (((1,), (1,)), ((), ())), preferred_element_type=jnp.float32
    )
    for copy in in_flight.values():
        copy.wait_send()


def second_layer(parts, keeps, messages, own, lists, counts, adj, w_self, w_neigh):
    plans = [plan_of(parts, share) for share in range(len(SHARES))]
    n_stages = len(plans[0])
    whole = pl.BlockSpec(memory_space=pltpu.VMEM)
    anywhere = pl.BlockSpec(memory_space=pl.ANY)
    rows, width = own.shape
    half = width // 2
    lengths = [length for _, length in SHARES]
    slots = lists.shape[1]
    buffers = [pltpu.VMEM(a.shape, jnp.float32) for a in keeps]
    for first_stage in (0, 1):
        for k in range(first_stage, n_stages):
            for share, n in enumerate(lengths):
                bits, stay, pieces, size = plans[share][k]
                buffers.append(pltpu.VMEM(((2 ** len(bits) - 1) * pieces, size * n + size, half), jnp.int32))
    chunk = max(chunk_of(parts), 8)
    buffers += [pltpu.VMEM((chunk, half), jnp.float32)] * 3
    buffers += [
        pltpu.VMEM(lists.shape[1:], jnp.int32),
        pltpu.VMEM((parts // 2 * slots, 2 * rows), jnp.bfloat16),
        pltpu.VMEM((rows, width), jnp.bfloat16),
        pltpu.VMEM((rows, width), jnp.bfloat16),
        pltpu.VMEM((parts // 2, 2 * slots, half), jnp.bfloat16),
        pltpu.VMEM((parts, 2 * slots, half), jnp.bfloat16),
        pltpu.VMEM((adj.shape[0], width), jnp.float32),
        pltpu.VMEM((adj.shape[0], width), jnp.float32),
    ]
    numbers = max(sum((2 ** len(p[0]) - 1) * p[2] for p in plan) for plan in plans)
    dma = pltpu.SemaphoreType.DMA
    buffers += [
        dma((len(SHARES) + 1,)),
        dma((len(SHARES), numbers)),
        dma((len(SHARES), numbers)),
        dma((2, 2)),
        dma((2,)),
    ]
    return pl.pallas_call(
        functools.partial(second_layer_kernel, parts),
        out_shape=jax.ShapeDtypeStruct((adj.shape[0], w_self.shape[0]), jnp.float32),
        in_specs=[anywhere] * 6 + [whole, anywhere] + [whole] * 4,
        out_specs=whole,
        scratch_shapes=buffers,
        compiler_params=pltpu.CompilerParams(
            collective_id=1, has_side_effects=True, vmem_limit_bytes=VMEM_LIMIT
        ),
        name="reduce_and_second_layer",
    )(*keeps, *messages, own, lists, counts, adj, w_self, w_neigh)


def body(
    features,
    tile_weight,
    tile_dst,
    tile_src,
    tile_rows,
    w_self1,
    neighbour_weight_first,
    send_list,
    send_count,
    adj_two,
    w_self2,
    w_neigh2,
):
    parts = lax.axis_size("dom")
    other, wn_other, ws_other = swap(features, neighbour_weight_first, w_self1)
    results = first_layer(
        parts,
        tile_dst,
        tile_src,
        tile_rows,
        features,
        other,
        neighbour_weight_first,
        wn_other,
        w_self1,
        ws_other,
        tile_weight,
    )
    return second_layer(parts, results[:3], results[3:6], results[6], send_list.transpose(0, 2, 1), send_count, adj_two, w_self2.T, w_neigh2.T)


def solution(mesh):
    in_specs = (
        P("dom", "feat"),
        P("dom", None, None),
        P("dom"),
        P("dom"),
        P("dom"),
        P("feat", None),
        P("feat", None),
        P(),
        P(),
        P("dom", None),
        P(),
        P(),
    )
    out_specs = P("dom", None)
    return jax.shard_map(body, mesh=mesh, in_specs=in_specs, out_specs=out_specs, check_vma=False)
```

```python
import functools

import jax
import jax.numpy as jnp
import numpy as np
from jax import lax
from jax.experimental import pallas as pl
from jax.experimental.pallas import tpu as pltpu
from jax.sharding import PartitionSpec as P

DIMS = {128: (4, 4, 8), 16: (4, 2, 2)}
SHARES = ((0, 24), (24, 24), (48, 16))


def stages_of(parts, share):
    bits = [[(axis, i) for i in range(bits_of(n))] for axis, n in enumerate(DIMS[parts])]
    x, y, z = bits
    if share == 0:
        return [x[:1], x[1:], y + z[:1], z[1:]] if len(z) > 1 else [x[:1], x[1:], y, z]
    if share == 1:
        return [y[:1], y[1:], x + z[:1], z[1:]] if len(y) > 1 else [y, x[:1], x[1:], z]
    return [z[:1], z[1:2], x[:1] + y[:1], x[1:] + y[1:] + z[2:]] if len(z) > 1 else [z, x[:1], x[1:], y]


GROUP = 4
GROUPS = 2
FIRST_VMEM = 52 * 1024 * 1024
SECOND_VMEM = 32 * 1024 * 1024
MESH = pl.DeviceIdType.MESH


def bits_of(count):
    return count.bit_length() - 1


def steps_of(parts, share):
    return [bit for stage in stages_of(parts, share) for bit in stage]


def chunk_of(parts):
    return parts // 8


def plan_of(parts, share):
    plan = []
    count = parts
    for bits in stages_of(parts, share):
        stay = count >> len(bits)
        size = min(stay, chunk_of(parts))
        plan.append((bits, stay, stay // size, size))
        count = stay
    return plan


@functools.lru_cache(maxsize=None)
def slot_table(parts):
    nx, ny, nz = DIMS[parts]
    table = np.zeros((2, len(SHARES), parts), np.int32)
    for f in range(2):
        for share in range(len(SHARES)):
            for b in range(parts):
                coords = (b % nx, b // nx % ny, b // (nx * ny))
                slot = 0
                for axis, i in steps_of(parts, share):
                    n = DIMS[parts][axis]
                    c = (coords[axis] - f) % n
                    slot = slot * 2 + ((c ^ (c >> 1)) >> i & 1)
                table[f, share, b] = slot
    return table


def place_of(parts, me):
    nx, ny, nz = DIMS[parts]
    return lax.rem(me, nx), lax.rem(lax.div(me, nx), ny), lax.div(me, nx * ny)


def chip_across(parts, me, f, bits):
    nx, ny, nz = DIMS[parts]
    place = place_of(parts, me)
    pitch = (1, nx, nx * ny)
    dom = me
    for axis, n in enumerate(DIMS[parts]):
        flips = sorted(i for a, i in bits if a == axis)
        if not flips:
            continue
        c = lax.rem(place[axis] - f + n, n)
        for i in flips:
            size = 2 ** (i + 1)
            c = c + (size - 1) - 2 * lax.rem(c, size)
        dom = dom + (lax.rem(c + f, n) - place[axis]) * pitch[axis]
    return dom


def swap_kernel(x_ref, wn_ref, ws_ref, xo_ref, wno_ref, wso_ref, send, recv):
    other = 1 - lax.axis_index("feat")
    barrier = pltpu.get_barrier_semaphore()
    pl.semaphore_signal(barrier, inc=1, device_id={"feat": other}, device_id_type=MESH)
    pl.semaphore_wait(barrier, 1)
    copies = []
    for k, (a, b) in enumerate(((x_ref, xo_ref), (wn_ref, wno_ref), (ws_ref, wso_ref))):
        copy = pltpu.make_async_remote_copy(
            src_ref=a,
            dst_ref=b,
            send_sem=send.at[k],
            recv_sem=recv.at[k],
            device_id={"feat": other},
            device_id_type=MESH,
        )
        copy.start()
        copies.append(copy)
    for copy in copies:
        copy.wait()


def swap(features, wn, ws):
    anywhere = pl.BlockSpec(memory_space=pl.ANY)
    return pl.pallas_call(
        swap_kernel,
        out_shape=[jax.ShapeDtypeStruct(a.shape, a.dtype) for a in (features, wn, ws)],
        in_specs=[anywhere] * 3,
        out_specs=[anywhere] * 3,
        scratch_shapes=[pltpu.SemaphoreType.DMA((3,)), pltpu.SemaphoreType.DMA((3,))],
        compiler_params=pltpu.CompilerParams(collective_id=0, has_side_effects=True),
        name="swap_halves",
    )(features, wn, ws)


def encode(load, count, rows, out, peak, inv):
    def largest(j, carry):
        v = jnp.abs(load(j))
        half = v.shape[1] // 2
        peak[pl.ds(j, 1), :] = jnp.max(jnp.maximum(v[:, :half], v[:, half:]), axis=0, keepdims=True)
        return carry

    lax.fori_loop(0, count, largest, 0, unroll=True)
    top = jnp.maximum(peak[:count, :], 1e-30)
    code = jnp.ceil(jnp.log2(top) * 256.0) + 1.0
    out[count * rows : count * rows + count, :] = code.astype(jnp.int32)
    inv[:count, :] = jnp.exp2(code * (-1.0 / 256.0)) * 32767.0

    def pack(j, carry):
        v = load(j)
        half = v.shape[1] // 2
        s = inv[pl.ds(j, 1), :]
        low = jnp.round(v[:, :half] * s).astype(jnp.int32)
        high = jnp.round(v[:, half:] * s).astype(jnp.int32)
        out[pl.ds(j * rows, rows), :] = jnp.bitwise_or(
            jnp.left_shift(high, 16), jnp.bitwise_and(low, 0xFFFF)
        )
        return carry

    lax.fori_loop(0, count, pack, 0, unroll=True)


def decode_add(src, total, rows, low, high, work, first, scale):
    count = high - low
    code = src[total * rows : total * rows + total, :].astype(jnp.float32)
    scale[:total, :] = jnp.exp2(code * (1.0 / 256.0)) * (1.0 / 32767.0)

    def add(j, carry):
        word = src[pl.ds((low + j) * rows, rows), :]
        s = scale[pl.ds(low + j, 1), :]
        a = jnp.right_shift(jnp.left_shift(word, 16), 16).astype(jnp.float32) * s
        b = jnp.right_shift(word, 16).astype(jnp.float32) * s
        half = a.shape[1]
        work[first + low + j, :, :half] += a
        work[first + low + j, :, half:] += b
        return carry

    lax.fori_loop(0, count, add, 0, unroll=True)


def first_layer_kernel(parts, *refs):
    table, dst, src, limit = refs[:4]
    inputs = refs[4:11]
    accs, sends, own = refs[11:14], refs[14:17], refs[17]
    held = refs[18:25]
    order, count, plan, gathered, peak, inv, load_sem = refs[25:]
    xa, xb, wa, wb, sa, sb, tiles = held
    f, me = lax.axis_index("feat"), lax.axis_index("dom")
    n_tiles, rows, size = tiles.shape
    blocks = xa.shape[0] // size
    half = parts // 2
    depth = xa.shape[1]
    group_rows = GROUP * rows

    loads = []
    for k in range(7):
        source = inputs[k].at[:, pl.ds(pl.multiple_of(f * rows, rows), rows), :] if k == 6 else inputs[k]
        copy = pltpu.make_async_copy(source, held[k], load_sem.at[k])
        copy.start()
        loads.append(copy)

    for s in range(blocks):
        count[s] = 0

    def place(t, carry):
        s = src[t]
        at = count[s]
        order[s, at] = t
        count[s] = at + 1
        return carry

    lax.fori_loop(0, n_tiles, place, 0)

    def groups_of(s, at):
        n = count[s]

        def one(g, at):
            plan[0, at] = s
            plan[1, at] = g * GROUP
            plan[2, at] = jnp.minimum(n - g * GROUP, GROUP)
            return at + 1

        return lax.fori_loop(0, lax.div(n + GROUP - 1, GROUP), one, at)

    n_groups = lax.fori_loop(0, blocks, groups_of, 0)
    for g in range(3 * GROUPS):
        plan[0, n_groups + g] = 0
        plan[1, n_groups + g] = 0
        plan[2, n_groups + g] = 0

    def clear(j, carry):
        for acc in accs:
            acc[j] = jnp.zeros(acc.shape[1:], jnp.float32)
        return carry

    lax.fori_loop(0, parts, clear, 0, unroll=4)
    for copy in loads:
        copy.wait()

    mine = pl.ds(pl.multiple_of(f * rows, rows), rows)
    own[...] = jnp.dot(xa[mine, :], sa[...], preferred_element_type=jnp.float32) + jnp.dot(
        xb[mine, :], sb[...], preferred_element_type=jnp.float32
    )
    row_ids = lax.broadcasted_iota(jnp.int32, (rows, size), 0) + f * rows
    bases = [table[f, share, me] for share in range(len(SHARES))]

    def gather(g, buffer):
        for u in range(GROUPS):
            s, first, n = plan[0, g + u], plan[1, g + u], plan[2, g + u]
            pieces = []
            for j in range(GROUP):
                valid = j < n
                t = jnp.where(valid, order[s, first + j], 0)
                tile = tiles[t]
                pieces.append(jnp.where(row_ids < jnp.where(valid, limit[t], 0), tile, jnp.zeros_like(tile)))
            a = jnp.concatenate(pieces, axis=0)
            at_source = pl.ds(pl.multiple_of(s * size, size), size)
            at = slice(u * group_rows, (u + 1) * group_rows)
            buffer[at, :depth] = jnp.dot(a, xa[at_source, :], preferred_element_type=jnp.float32).astype(
                jnp.bfloat16
            )
            buffer[at, depth:] = jnp.dot(a, xb[at_source, :], preferred_element_type=jnp.float32).astype(
                jnp.bfloat16
            )

    def spread(g, buffer):
        h = jnp.dot(buffer[:, :depth], wa[...], preferred_element_type=jnp.float32) + jnp.dot(
            buffer[:, depth:], wb[...], preferred_element_type=jnp.float32
        )
        for u in range(GROUPS):
            s, first, n = plan[0, g + u], plan[1, g + u], plan[2, g + u]
            for j in range(GROUP):
                d = dst[jnp.where(j < n, order[s, first + j], 0)]
                for share, (start, length) in enumerate(SHARES):
                    slot = jnp.bitwise_xor(table[f, share, d], bases[share])
                    at = (u * GROUP + j) * rows + start
                    accs[share][slot] += h[at : at + length, :]

    gather(0, gathered.at[0])

    def step(i, carry):
        g = i * (2 * GROUPS)
        spread(g, gathered.at[0])
        gather(g + GROUPS, gathered.at[1])
        spread(g + GROUPS, gathered.at[1])
        gather(g + 2 * GROUPS, gathered.at[0])
        return carry

    lax.fori_loop(0, lax.div(n_groups + 2 * GROUPS - 1, 2 * GROUPS), step, 0)

    chunk = chunk_of(parts)
    pieces = half // chunk
    for piece in range(pieces):
        for share, (start, length) in enumerate(SHARES):
            acc = accs[share]
            first = half + (pieces - 1 - piece) * chunk
            encode(lambda j: acc[first + j], chunk, length, sends[share].at[piece], peak, inv)


def first_layer(parts, dst, src, limit, features, other, wn, wn_other, ws, ws_other, tiles):
    n_tiles, size, _ = tiles.shape
    rows = size // 2
    width = wn.shape[1]
    half = parts // 2
    chunk = chunk_of(parts)
    pieces = half // chunk
    scalars = pl.BlockSpec(memory_space=pltpu.SMEM)
    anywhere = pl.BlockSpec(memory_space=pl.ANY)
    lengths = [length for _, length in SHARES]
    message = [(pieces, chunk * n + chunk, width // 2) for n in lengths]
    operands = (features, other, wn, wn_other, ws, ws_other)
    blocks = features.shape[0] // size
    return pl.pallas_call(
        functools.partial(first_layer_kernel, parts),
        in_specs=[scalars] * 4 + [anywhere] * 7,
        out_specs=[pl.BlockSpec(memory_space=pltpu.VMEM)] * 7,
        scratch_shapes=[pltpu.VMEM(a.shape, a.dtype) for a in operands]
        + [
            pltpu.VMEM((n_tiles, rows, size), tiles.dtype),
            pltpu.SMEM((blocks, n_tiles + GROUP), jnp.int32),
            pltpu.SMEM((blocks,), jnp.int32),
            pltpu.SMEM((3, n_tiles // GROUP + blocks + 3 * GROUPS), jnp.int32),
            pltpu.VMEM((2, GROUPS * GROUP * rows, 2 * features.shape[1]), jnp.bfloat16),
            pltpu.VMEM((max(chunk, 8), width // 2), jnp.float32),
            pltpu.VMEM((max(chunk, 8), width // 2), jnp.float32),
            pltpu.SemaphoreType.DMA((7,)),
        ],
        out_shape=[pltpu.VMEM((parts, n, width), jnp.float32) for n in lengths]
        + [pltpu.VMEM(shape, jnp.int32) for shape in message]
        + [pltpu.VMEM((rows, width), jnp.float32)],
        compiler_params=pltpu.CompilerParams(vmem_limit_bytes=FIRST_VMEM),
        name="first_layer",
    )(jnp.asarray(slot_table(parts)), dst, src, limit, *operands, tiles)


def second_layer_kernel(parts, *refs):
    nx, ny, nz = DIMS[parts]
    plane = nx * ny
    n_shares = len(SHARES)
    plans = [plan_of(parts, share) for share in range(n_shares)]
    n_stages = len(plans[0])
    keeps, messages = refs[0:3], refs[3:6]
    own_ref, list_ref, count_hbm, adj_hbm, w_self_hbm, w_neigh_hbm, out_ref = refs[6:13]
    at = 13
    work = refs[at : at + 3]
    at += 3
    receive, outgoing = [], []
    for k in range(n_stages):
        receive.append(refs[at : at + 3])
        at += 3
    for k in range(n_stages):
        outgoing.append(refs[at : at + 3] if k > 0 else None)
        at += 3 if k > 0 else 0
    (peak, inv, scale, lists, onehot, hid_own, hid_other, rows_out, rows_in, part, part_other) = refs[at : at + 11]
    count_ref, adj_ref, w_self_ref, w_neigh_ref = refs[at + 11 : at + 15]
    local_sem, send_sem, recv_sem, pair_sem, rows_sem = refs[at + 15 :]

    f = lax.axis_index("feat")
    me = lax.axis_index("dom")
    partners = {}
    for share in range(n_shares):
        for k, (bits, stay, pieces, size) in enumerate(plans[share]):
            for mask in range(1, 2 ** len(bits)):
                chosen = tuple(sorted(b for i, b in enumerate(bits) if mask >> (len(bits) - 1 - i) & 1))
                if chosen not in partners:
                    partners[chosen] = chip_across(parts, me, f, chosen)
    rows_in[...] = jnp.zeros_like(rows_in)
    barrier = pltpu.get_barrier_semaphore()
    for target in [{"feat": 1 - f}] + [{"dom": dom} for dom in partners.values()]:
        pl.semaphore_signal(barrier, inc=1, device_id=target, device_id_type=MESH)
    pl.semaphore_wait(barrier, 1 + len(partners))

    def message(k, share, mask, piece, src):
        bits, stay, pieces, size = plans[share][k]
        index = (mask - 1) * pieces + piece
        number = sum((2 ** len(p[0]) - 1) * p[2] for p in plans[share][:k]) + index
        chosen = tuple(sorted(b for i, b in enumerate(bits) if mask >> (len(bits) - 1 - i) & 1))
        return pltpu.make_async_remote_copy(
            src_ref=src,
            dst_ref=receive[k][share].at[index],
            send_sem=send_sem.at[share, number],
            recv_sem=recv_sem.at[share, number],
            device_id={"dom": partners[chosen]},
            device_id_type=MESH,
        )

    in_flight = {}
    for piece in range(plans[0][0][2]):
        for share in range(n_shares):
            copy = message(0, share, 1, piece, messages[share].at[piece])
            copy.start()
            in_flight[0, share, 1, piece] = copy
    loads = []
    for share in range(n_shares):
        copy = pltpu.make_async_copy(keeps[share].at[pl.ds(0, parts // 2)], work[share], local_sem.at[share])
        copy.start()
        loads.append(copy)

    get_lists = pltpu.make_async_copy(list_ref.at[me], lists, local_sem.at[len(SHARES)])
    get_lists.start()
    loads.append(get_lists)
    late = ((count_hbm, count_ref), (adj_hbm, adj_ref), (w_self_hbm, w_self_ref), (w_neigh_hbm, w_neigh_ref))
    for k, (source, target) in enumerate(late):
        copy = pltpu.make_async_copy(source, target, local_sem.at[len(SHARES) + 1 + k])
        copy.start()
        loads.append(copy)
    for copy in loads:
        copy.wait()
    slots = lists.shape[0]
    shape = lists.shape
    lanes = lax.broadcasted_iota(jnp.int32, shape, 1)
    valid = lax.broadcasted_iota(jnp.int32, shape, 0) < count_ref[pl.ds(me, 1), :]
    wanted = jnp.where(valid, lists[...], -1).astype(jnp.float32)
    hidden_rows = onehot.shape[1]
    ids = lax.broadcasted_iota(jnp.int32, (slots, hidden_rows), 1).astype(jnp.float32)
    px, py, pz = place_of(parts, me)
    at_x = [lax.rem(px + d, nx) for d in range(nx)]
    at_y = [lax.rem(py + d, ny) * nx for d in range(ny)]
    at_z = [lax.rem(pz + d, nz) * (nx * ny) for d in range(nz)]
    receivers = []
    for d in [0] + sorted(range(1, nz // 2), key=lambda d: -min(2 * d, nz - 2 * d)):
        by_parity = [jnp.where(f == odd, at_z[2 * d], at_z[2 * d + 1]) for odd in range(2)]
        for dy in range(ny):
            for dx in range(nx):
                receivers.append(at_x[dx] + at_y[dy] + by_parity[(dx + dy) % 2])

    for i in range(0, len(receivers), 2):
        pair = []
        for r in receivers[i : i + 2]:
            column = jnp.sum(jnp.where(lanes == r, wanted, 0.0), axis=1, keepdims=True)
            pair.append(jnp.where(column == ids, 1.0, 0.0))
        onehot[i * slots : (i + 2) * slots, :] = jnp.concatenate(pair, axis=0).astype(jnp.bfloat16)

    def absorb(k, share, mask, piece, low, high):
        bits, stay, pieces, size = plans[share][k]
        first = (pieces - 1 - piece) * size
        source = receive[k][share].at[(mask - 1) * pieces + piece]
        decode_add(source, size, SHARES[share][1], low - first, high - first, work[share], first, scale)

    def forward(k, share, mask, piece):
        bits, stay, pieces, size = plans[share][k]
        first = mask * stay + (pieces - 1 - piece) * size
        out = outgoing[k][share].at[(mask - 1) * pieces + piece]
        encode(lambda j: work[share][first + j], size, SHARES[share][1], out, peak, inv)
        copy = message(k, share, mask, piece, out)
        copy.start()
        in_flight[k, share, mask, piece] = copy

    for k in range(n_stages):
        for piece in range(plans[0][k][2]):
            for share in reversed(range(n_shares)):
                bits, stay, pieces, size = plans[share][k]
                masks = range(1, 2 ** len(bits))
                for mask in masks:
                    in_flight[k, share, mask, piece].wait_recv()
                top = (pieces - piece) * size
                bottom = top - size
                leaving = []
                if k + 1 < n_stages:
                    next_bits, next_stay, next_pieces, next_size = plans[share][k + 1]
                    for mask in reversed(range(1, 2 ** len(next_bits))):
                        for next_piece in range(next_pieces):
                            low = mask * next_stay + (next_pieces - 1 - next_piece) * next_size
                            if bottom <= low < top:
                                leaving.append((low, low + next_size, mask, next_piece))
                for low, high, mask, next_piece in leaving:
                    for m in masks:
                        absorb(k, share, m, piece, low, high)
                    forward(k + 1, share, mask, next_piece)
                rest = min([low for low, *_ in leaving] + [top])
                if rest > bottom:
                    for m in masks:
                        absorb(k, share, m, piece, bottom, rest)

    for share, (start, length) in enumerate(SHARES):
        total = work[share][0] + own_ref[start : start + length, :]
        work[share][0] = jnp.maximum(total, 0.0)
    hid_own[...] = jnp.concatenate([work[share][0] for share in range(n_shares)], axis=0).astype(jnp.bfloat16)

    def to_pair(src, dst, number):
        return pltpu.make_async_remote_copy(
            src_ref=src,
            dst_ref=dst,
            send_sem=pair_sem.at[0, number],
            recv_sem=pair_sem.at[1, number],
            device_id={"feat": 1 - f},
            device_id_type=MESH,
        )

    share_hidden = to_pair(hid_own, hid_other, 0)
    share_hidden.start()
    share_hidden.wait()
    mine, theirs = hid_own[...], hid_other[...]
    hidden = jnp.concatenate([jnp.where(f == 0, mine, theirs), jnp.where(f == 0, theirs, mine)], axis=0)
    width = hidden.shape[1] // 2
    picked = jnp.dot(onehot[...], hidden, preferred_element_type=jnp.float32)
    for i in range(len(receivers)):
        block = picked[i * slots : (i + 1) * slots, :]
        rows_out[i] = jnp.concatenate([block[:, :width], block[:, width:]], axis=0).astype(jnp.bfloat16)

    def to_receiver(i):
        return pltpu.make_async_remote_copy(
            src_ref=rows_out.at[i],
            dst_ref=rows_in.at[me],
            send_sem=rows_sem.at[0],
            recv_sem=rows_sem.at[1],
            device_id={"dom": receivers[i]},
            device_id_type=MESH,
        )

    near = nx * ny
    for i in list(range(near, len(receivers))) + list(range(1, near)):
        to_receiver(i).start()

    @pl.when(f == 0)
    def _():
        rows_in[me] = rows_out[0]

    @pl.when(f == 1)
    def _():
        to_receiver(0).start()

    n_own = hidden.shape[0]
    out_rows = out_ref.shape[0]
    own_total = jnp.dot(adj_ref[:, :n_own], hidden, preferred_element_type=jnp.float32)
    self_logits = lax.dot_general(
        hidden[:out_rows], w_self_ref[...], (((1,), (1,)), ((), ())), preferred_element_type=jnp.float32
    )
    blocks = len(receivers)

    def wait_rows(n):
        for number, ref in ((0, rows_out), (1, rows_in)):
            pltpu.make_async_copy(ref.at[pl.ds(0, n)], ref.at[pl.ds(0, n)], rows_sem.at[number]).wait()

    pl.when(f == 0)(lambda: wait_rows(blocks - 1))
    pl.when(f == 1)(lambda: wait_rows(blocks))

    arrived = rows_in[...].astype(jnp.float32)
    pool = [
        arrived[:, k * slots : (k + 1) * slots, :].reshape(parts * slots, width).astype(jnp.bfloat16)
        for k in range(2)
    ]
    for k in range(2):
        part[:, k * width : (k + 1) * width] = jnp.dot(
            adj_ref[:, n_own:], pool[k], preferred_element_type=jnp.float32
        )
    share_part = to_pair(part, part_other, 1)
    share_part.start()
    share_part.wait()
    aggregate = (part[...] + part_other[...] + own_total).astype(jnp.bfloat16)
    out_ref[...] = self_logits + lax.dot_general(
        aggregate, w_neigh_ref[...], (((1,), (1,)), ((), ())), preferred_element_type=jnp.float32
    )
    for copy in in_flight.values():
        copy.wait_send()


def second_layer(parts, keeps, messages, own, lists, counts, adj, w_self, w_neigh):
    plans = [plan_of(parts, share) for share in range(len(SHARES))]
    n_stages = len(plans[0])
    whole = pl.BlockSpec(memory_space=pltpu.VMEM)
    anywhere = pl.BlockSpec(memory_space=pl.ANY)
    rows, width = own.shape
    half = width // 2
    lengths = [length for _, length in SHARES]
    slots = lists.shape[1]
    buffers = [pltpu.VMEM((parts // 2,) + a.shape[1:], jnp.float32) for a in keeps]
    for first_stage in (0, 1):
        for k in range(first_stage, n_stages):
            for share, n in enumerate(lengths):
                bits, stay, pieces, size = plans[share][k]
                buffers.append(pltpu.VMEM(((2 ** len(bits) - 1) * pieces, size * n + size, half), jnp.int32))
    chunk = max(chunk_of(parts), 8)
    buffers += [pltpu.VMEM((chunk, half), jnp.float32)] * 3
    buffers += [
        pltpu.VMEM(lists.shape[1:], jnp.int32),
        pltpu.VMEM((parts // 2 * slots, 2 * rows), jnp.bfloat16),
        pltpu.VMEM((rows, width), jnp.bfloat16),
        pltpu.VMEM((rows, width), jnp.bfloat16),
        pltpu.VMEM((parts // 2, 2 * slots, half), jnp.bfloat16),
        pltpu.VMEM((parts, 2 * slots, half), jnp.bfloat16),
        pltpu.VMEM((adj.shape[0], width), jnp.float32),
        pltpu.VMEM((adj.shape[0], width), jnp.float32),
        pltpu.VMEM(counts.shape, counts.dtype),
        pltpu.VMEM(adj.shape, adj.dtype),
        pltpu.VMEM(w_self.shape, w_self.dtype),
        pltpu.VMEM(w_neigh.shape, w_neigh.dtype),
    ]
    numbers = max(sum((2 ** len(p[0]) - 1) * p[2] for p in plan) for plan in plans)
    dma = pltpu.SemaphoreType.DMA
    buffers += [
        dma((len(SHARES) + 5,)),
        dma((len(SHARES), numbers)),
        dma((len(SHARES), numbers)),
        dma((2, 2)),
        dma((2,)),
    ]
    return pl.pallas_call(
        functools.partial(second_layer_kernel, parts),
        out_shape=jax.ShapeDtypeStruct((adj.shape[0], w_self.shape[0]), jnp.float32),
        in_specs=[whole] * 7 + [anywhere] * 5,
        out_specs=whole,
        scratch_shapes=buffers,
        compiler_params=pltpu.CompilerParams(
            collective_id=1, has_side_effects=True, vmem_limit_bytes=SECOND_VMEM
        ),
        name="reduce_and_second_layer",
    )(*keeps, *messages, own, lists, counts, adj, w_self, w_neigh)


def body(
    features,
    tile_weight,
    tile_dst,
    tile_src,
    tile_rows,
    w_self1,
    neighbour_weight_first,
    send_list,
    send_count,
    adj_two,
    w_self2,
    w_neigh2,
):
    parts = lax.axis_size("dom")
    other, wn_other, ws_other = swap(features, neighbour_weight_first, w_self1)
    results = first_layer(
        parts,
        tile_dst,
        tile_src,
        tile_rows,
        features,
        other,
        neighbour_weight_first,
        wn_other,
        w_self1,
        ws_other,
        tile_weight,
    )
    return second_layer(parts, results[:3], results[3:6], results[6], send_list.transpose(0, 2, 1), send_count, adj_two, w_self2.T, w_neigh2.T)


def solution(mesh):
    in_specs = (
        P("dom", "feat"),
        P("dom", None, None),
        P("dom"),
        P("dom"),
        P("dom"),
        P("feat", None),
        P("feat", None),
        P(),
        P(),
        P("dom", None),
        P(),
        P(),
    )
    out_specs = P("dom", None)
    return jax.shard_map(body, mesh=mesh, in_specs=in_specs, out_specs=out_specs, check_vma=False)
```

```python
import functools

import jax
import jax.numpy as jnp
import numpy as np
from jax import lax
from jax.experimental import pallas as pl
from jax.experimental.pallas import tpu as pltpu
from jax.sharding import PartitionSpec as P

DIMS = {128: (4, 4, 8), 16: (4, 2, 2)}
SHARES = ((0, 24), (24, 24), (48, 16))


def stages_of(parts, share):
    bits = [[(axis, i) for i in range(bits_of(n))] for axis, n in enumerate(DIMS[parts])]
    x, y, z = bits
    if share == 0:
        return [x[:1], x[1:], y + z[:1], z[1:]] if len(z) > 1 else [x[:1], x[1:], y, z]
    if share == 1:
        return [y[:1], y[1:], x + z[:1], z[1:]] if len(y) > 1 else [y, x[:1], x[1:], z]
    return [z[:1], z[1:2], x[:1] + y[:1], x[1:] + y[1:] + z[2:]] if len(z) > 1 else [z, x[:1], x[1:], y]


GROUP = 4
GROUPS = 2
FIRST_VMEM = 52 * 1024 * 1024
SECOND_VMEM = 32 * 1024 * 1024
MESH = pl.DeviceIdType.MESH


def bits_of(count):
    return count.bit_length() - 1


def steps_of(parts, share):
    return [bit for stage in stages_of(parts, share) for bit in stage]


def chunk_of(parts):
    return parts // 8


def plan_of(parts, share):
    plan = []
    count = parts
    for bits in stages_of(parts, share):
        stay = count >> len(bits)
        size = min(stay, chunk_of(parts))
        plan.append((bits, stay, stay // size, size))
        count = stay
    return plan


@functools.lru_cache(maxsize=None)
def slot_table(parts):
    nx, ny, nz = DIMS[parts]
    table = np.zeros((2, len(SHARES), parts), np.int32)
    for f in range(2):
        for share in range(len(SHARES)):
            for b in range(parts):
                coords = (b % nx, b // nx % ny, b // (nx * ny))
                slot = 0
                for axis, i in steps_of(parts, share):
                    n = DIMS[parts][axis]
                    c = (coords[axis] - f) % n
                    slot = slot * 2 + ((c ^ (c >> 1)) >> i & 1)
                table[f, share, b] = slot
    return table


def place_of(parts, me):
    nx, ny, nz = DIMS[parts]
    return lax.rem(me, nx), lax.rem(lax.div(me, nx), ny), lax.div(me, nx * ny)


def chip_across(parts, me, f, bits):
    nx, ny, nz = DIMS[parts]
    place = place_of(parts, me)
    pitch = (1, nx, nx * ny)
    dom = me
    for axis, n in enumerate(DIMS[parts]):
        flips = sorted(i for a, i in bits if a == axis)
        if not flips:
            continue
        c = lax.rem(place[axis] - f + n, n)
        for i in flips:
            size = 2 ** (i + 1)
            c = c + (size - 1) - 2 * lax.rem(c, size)
        dom = dom + (lax.rem(c + f, n) - place[axis]) * pitch[axis]
    return dom


def swap_kernel(x_ref, wn_ref, ws_ref, xo_ref, wno_ref, wso_ref, send, recv):
    other = 1 - lax.axis_index("feat")
    barrier = pltpu.get_barrier_semaphore()
    pl.semaphore_signal(barrier, inc=1, device_id={"feat": other}, device_id_type=MESH)
    pl.semaphore_wait(barrier, 1)
    copies = []
    for k, (a, b) in enumerate(((x_ref, xo_ref), (wn_ref, wno_ref), (ws_ref, wso_ref))):
        copy = pltpu.make_async_remote_copy(
            src_ref=a,
            dst_ref=b,
            send_sem=send.at[k],
            recv_sem=recv.at[k],
            device_id={"feat": other},
            device_id_type=MESH,
        )
        copy.start()
        copies.append(copy)
    for copy in copies:
        copy.wait()


def swap(features, wn, ws):
    anywhere = pl.BlockSpec(memory_space=pl.ANY)
    return pl.pallas_call(
        swap_kernel,
        out_shape=[jax.ShapeDtypeStruct(a.shape, a.dtype) for a in (features, wn, ws)],
        in_specs=[anywhere] * 3,
        out_specs=[anywhere] * 3,
        scratch_shapes=[pltpu.SemaphoreType.DMA((3,)), pltpu.SemaphoreType.DMA((3,))],
        compiler_params=pltpu.CompilerParams(collective_id=0, has_side_effects=True),
        name="swap_halves",
    )(features, wn, ws)


def encode(load, count, rows, out, peak, inv):
    def largest(j, carry):
        v = jnp.abs(load(j))
        half = v.shape[1] // 2
        peak[pl.ds(j, 1), :] = jnp.max(jnp.maximum(v[:, :half], v[:, half:]), axis=0, keepdims=True)
        return carry

    lax.fori_loop(0, count, largest, 0, unroll=True)
    top = jnp.maximum(peak[:count, :], 1e-30)
    code = jnp.ceil(jnp.log2(top) * 256.0) + 1.0
    out[count * rows : count * rows + count, :] = code.astype(jnp.int32)
    inv[:count, :] = jnp.exp2(code * (-1.0 / 256.0)) * 32767.0

    def pack(j, carry):
        v = load(j)
        half = v.shape[1] // 2
        s = inv[pl.ds(j, 1), :]
        low = jnp.round(v[:, :half] * s).astype(jnp.int32)
        high = jnp.round(v[:, half:] * s).astype(jnp.int32)
        out[pl.ds(j * rows, rows), :] = jnp.bitwise_or(
            jnp.left_shift(high, 16), jnp.bitwise_and(low, 0xFFFF)
        )
        return carry

    lax.fori_loop(0, count, pack, 0, unroll=True)


def decode_add(src, total, rows, low, high, work, first, scale):
    count = high - low
    code = src[total * rows : total * rows + total, :].astype(jnp.float32)
    scale[:total, :] = jnp.exp2(code * (1.0 / 256.0)) * (1.0 / 32767.0)

    def add(j, carry):
        word = src[pl.ds((low + j) * rows, rows), :]
        s = scale[pl.ds(low + j, 1), :]
        a = jnp.right_shift(jnp.left_shift(word, 16), 16).astype(jnp.float32) * s
        b = jnp.right_shift(word, 16).astype(jnp.float32) * s
        half = a.shape[1]
        work[first + low + j, :, :half] += a
        work[first + low + j, :, half:] += b
        return carry

    lax.fori_loop(0, count, add, 0, unroll=True)


def first_layer_kernel(parts, *refs):
    table, dst, src, limit = refs[:4]
    inputs = refs[4:11]
    accs, sends, own = refs[11:14], refs[14:17], refs[17]
    held = refs[18:25]
    order, count, plan, gathered, peak, inv, load_sem = refs[25:]
    xa, xb, wa, wb, sa, sb, tiles = held
    f, me = lax.axis_index("feat"), lax.axis_index("dom")
    n_tiles, rows, size = tiles.shape
    blocks = xa.shape[0] // size
    half = parts // 2
    depth = xa.shape[1]
    group_rows = GROUP * rows

    loads = []
    for k in range(7):
        source = inputs[k].at[:, pl.ds(pl.multiple_of(f * rows, rows), rows), :] if k == 6 else inputs[k]
        copy = pltpu.make_async_copy(source, held[k], load_sem.at[k])
        copy.start()
        loads.append(copy)

    for s in range(blocks):
        count[s] = 0

    def place(t, carry):
        s = src[t]
        at = count[s]
        order[s, at] = t
        count[s] = at + 1
        clear(t)
        return carry

    def clear(j):
        for acc in accs:
            acc[j] = jnp.zeros(acc.shape[1:], jnp.float32)

    lax.fori_loop(0, n_tiles, place, 0)
    for j in range(n_tiles, parts):
        clear(j)

    def groups_of(s, at):
        n = count[s]

        def one(g, at):
            plan[0, at] = s
            plan[1, at] = g * GROUP
            plan[2, at] = jnp.minimum(n - g * GROUP, GROUP)
            return at + 1

        return lax.fori_loop(0, lax.div(n + GROUP - 1, GROUP), one, at)

    n_groups = lax.fori_loop(0, blocks, groups_of, 0)
    for g in range(3 * GROUPS):
        plan[0, n_groups + g] = 0
        plan[1, n_groups + g] = 0
        plan[2, n_groups + g] = 0

    for copy in loads:
        copy.wait()

    mine = pl.ds(pl.multiple_of(f * rows, rows), rows)
    own[...] = jnp.dot(xa[mine, :], sa[...], preferred_element_type=jnp.float32) + jnp.dot(
        xb[mine, :], sb[...], preferred_element_type=jnp.float32
    )
    row_ids = lax.broadcasted_iota(jnp.int32, (rows, size), 0) + f * rows
    bases = [table[f, share, me] for share in range(len(SHARES))]

    def gather(g, buffer):
        for u in range(GROUPS):
            s, first, n = plan[0, g + u], plan[1, g + u], plan[2, g + u]
            pieces = []
            for j in range(GROUP):
                valid = j < n
                t = jnp.where(valid, order[s, first + j], 0)
                tile = tiles[t]
                pieces.append(jnp.where(row_ids < jnp.where(valid, limit[t], 0), tile, jnp.zeros_like(tile)))
            a = jnp.concatenate(pieces, axis=0)
            at_source = pl.ds(pl.multiple_of(s * size, size), size)
            at = slice(u * group_rows, (u + 1) * group_rows)
            buffer[at, :depth] = jnp.dot(a, xa[at_source, :], preferred_element_type=jnp.float32).astype(
                jnp.bfloat16
            )
            buffer[at, depth:] = jnp.dot(a, xb[at_source, :], preferred_element_type=jnp.float32).astype(
                jnp.bfloat16
            )

    def spread(g, buffer):
        h = jnp.dot(buffer[:, :depth], wa[...], preferred_element_type=jnp.float32) + jnp.dot(
            buffer[:, depth:], wb[...], preferred_element_type=jnp.float32
        )
        for u in range(GROUPS):
            s, first, n = plan[0, g + u], plan[1, g + u], plan[2, g + u]
            for j in range(GROUP):
                d = dst[jnp.where(j < n, order[s, first + j], 0)]
                for share, (start, length) in enumerate(SHARES):
                    slot = jnp.bitwise_xor(table[f, share, d], bases[share])
                    at = (u * GROUP + j) * rows + start
                    accs[share][slot] += h[at : at + length, :]

    gather(0, gathered.at[0])

    def step(i, carry):
        g = i * (2 * GROUPS)
        spread(g, gathered.at[0])
        gather(g + GROUPS, gathered.at[1])
        spread(g + GROUPS, gathered.at[1])
        gather(g + 2 * GROUPS, gathered.at[0])
        return carry

    lax.fori_loop(0, lax.div(n_groups + 2 * GROUPS - 1, 2 * GROUPS), step, 0)

    chunk = chunk_of(parts)
    pieces = half // chunk
    for piece in range(pieces):
        for share, (start, length) in enumerate(SHARES):
            acc = accs[share]
            first = half + (pieces - 1 - piece) * chunk
            encode(lambda j: acc[first + j], chunk, length, sends[share].at[piece], peak, inv)


def first_layer(parts, dst, src, limit, features, other, wn, wn_other, ws, ws_other, tiles):
    n_tiles, size, _ = tiles.shape
    rows = size // 2
    width = wn.shape[1]
    half = parts // 2
    chunk = chunk_of(parts)
    pieces = half // chunk
    scalars = pl.BlockSpec(memory_space=pltpu.SMEM)
    anywhere = pl.BlockSpec(memory_space=pl.ANY)
    lengths = [length for _, length in SHARES]
    message = [(pieces, chunk * n + chunk, width // 2) for n in lengths]
    operands = (features, other, wn, wn_other, ws, ws_other)
    blocks = features.shape[0] // size
    return pl.pallas_call(
        functools.partial(first_layer_kernel, parts),
        in_specs=[scalars] * 4 + [anywhere] * 7,
        out_specs=[pl.BlockSpec(memory_space=pltpu.VMEM)] * 7,
        scratch_shapes=[pltpu.VMEM(a.shape, a.dtype) for a in operands]
        + [
            pltpu.VMEM((n_tiles, rows, size), tiles.dtype),
            pltpu.SMEM((blocks, n_tiles + GROUP), jnp.int32),
            pltpu.SMEM((blocks,), jnp.int32),
            pltpu.SMEM((3, n_tiles // GROUP + blocks + 3 * GROUPS), jnp.int32),
            pltpu.VMEM((2, GROUPS * GROUP * rows, 2 * features.shape[1]), jnp.bfloat16),
            pltpu.VMEM((max(chunk, 8), width // 2), jnp.float32),
            pltpu.VMEM((max(chunk, 8), width // 2), jnp.float32),
            pltpu.SemaphoreType.DMA((7,)),
        ],
        out_shape=[pltpu.VMEM((parts, n, width), jnp.float32) for n in lengths]
        + [pltpu.VMEM(shape, jnp.int32) for shape in message]
        + [pltpu.VMEM((rows, width), jnp.float32)],
        compiler_params=pltpu.CompilerParams(vmem_limit_bytes=FIRST_VMEM),
        name="first_layer",
    )(jnp.asarray(slot_table(parts)), dst, src, limit, *operands, tiles)


def second_layer_kernel(parts, *refs):
    nx, ny, nz = DIMS[parts]
    plane = nx * ny
    n_shares = len(SHARES)
    plans = [plan_of(parts, share) for share in range(n_shares)]
    n_stages = len(plans[0])
    keeps, messages = refs[0:3], refs[3:6]
    own_ref, list_ref, count_hbm, adj_hbm, w_self_hbm, w_neigh_hbm, out_ref = refs[6:13]
    at = 13
    work = refs[at : at + 3]
    at += 3
    receive, outgoing = [], []
    for k in range(n_stages):
        receive.append(refs[at : at + 3])
        at += 3
    for k in range(n_stages):
        outgoing.append(refs[at : at + 3] if k > 0 else None)
        at += 3 if k > 0 else 0
    (peak, inv, scale, lists, onehot, hid_own, hid_other, rows_out, rows_in, part, part_other) = refs[at : at + 11]
    count_ref, adj_ref, w_self_ref, w_neigh_ref = refs[at + 11 : at + 15]
    local_sem, send_sem, recv_sem, pair_sem, rows_sem = refs[at + 15 :]

    f = lax.axis_index("feat")
    me = lax.axis_index("dom")
    partners = {}
    for share in range(n_shares):
        for k, (bits, stay, pieces, size) in enumerate(plans[share]):
            for mask in range(1, 2 ** len(bits)):
                chosen = tuple(sorted(b for i, b in enumerate(bits) if mask >> (len(bits) - 1 - i) & 1))
                if chosen not in partners:
                    partners[chosen] = chip_across(parts, me, f, chosen)
    barrier = pltpu.get_barrier_semaphore()
    for target in [{"feat": 1 - f}] + [{"dom": dom} for dom in partners.values()]:
        pl.semaphore_signal(barrier, inc=1, device_id=target, device_id_type=MESH)
    rows_in[...] = jnp.zeros_like(rows_in)
    pl.semaphore_wait(barrier, 1 + len(partners))

    def message(k, share, mask, piece, src):
        bits, stay, pieces, size = plans[share][k]
        index = (mask - 1) * pieces + piece
        number = sum((2 ** len(p[0]) - 1) * p[2] for p in plans[share][:k]) + index
        chosen = tuple(sorted(b for i, b in enumerate(bits) if mask >> (len(bits) - 1 - i) & 1))
        return pltpu.make_async_remote_copy(
            src_ref=src,
            dst_ref=receive[k][share].at[index],
            send_sem=send_sem.at[share, number],
            recv_sem=recv_sem.at[share, number],
            device_id={"dom": partners[chosen]},
            device_id_type=MESH,
        )

    in_flight = {}
    for piece in range(plans[0][0][2]):
        for share in range(n_shares):
            copy = message(0, share, 1, piece, messages[share].at[piece])
            copy.start()
            in_flight[0, share, 1, piece] = copy
    loads = []
    for share in range(n_shares):
        copy = pltpu.make_async_copy(keeps[share].at[pl.ds(0, parts // 2)], work[share], local_sem.at[share])
        copy.start()
        loads.append(copy)

    get_lists = pltpu.make_async_copy(list_ref.at[me], lists, local_sem.at[len(SHARES)])
    get_lists.start()
    loads.append(get_lists)
    late = ((count_hbm, count_ref), (adj_hbm, adj_ref), (w_self_hbm, w_self_ref), (w_neigh_hbm, w_neigh_ref))
    for k, (source, target) in enumerate(late):
        copy = pltpu.make_async_copy(source, target, local_sem.at[len(SHARES) + 1 + k])
        copy.start()
        loads.append(copy)
    for copy in loads:
        copy.wait()
    slots = lists.shape[0]
    shape = lists.shape
    lanes = lax.broadcasted_iota(jnp.int32, shape, 1)
    valid = lax.broadcasted_iota(jnp.int32, shape, 0) < count_ref[pl.ds(me, 1), :]
    wanted = jnp.where(valid, lists[...], -1).astype(jnp.float32)
    hidden_rows = onehot.shape[1]
    ids = lax.broadcasted_iota(jnp.int32, (slots, hidden_rows), 1).astype(jnp.float32)
    px, py, pz = place_of(parts, me)
    at_x = [lax.rem(px + d, nx) for d in range(nx)]
    at_y = [lax.rem(py + d, ny) * nx for d in range(ny)]
    at_z = [lax.rem(pz + d, nz) * (nx * ny) for d in range(nz)]
    receivers = []
    for d in [0] + sorted(range(1, nz // 2), key=lambda d: -min(2 * d, nz - 2 * d)):
        by_parity = [jnp.where(f == odd, at_z[2 * d], at_z[2 * d + 1]) for odd in range(2)]
        for dy in range(ny):
            for dx in range(nx):
                receivers.append(at_x[dx] + at_y[dy] + by_parity[(dx + dy) % 2])

    for i in range(0, len(receivers), 2):
        pair = []
        for r in receivers[i : i + 2]:
            column = jnp.sum(jnp.where(lanes == r, wanted, 0.0), axis=1, keepdims=True)
            pair.append(jnp.where(column == ids, 1.0, 0.0))
        onehot[i * slots : (i + 2) * slots, :] = jnp.concatenate(pair, axis=0).astype(jnp.bfloat16)

    def absorb(k, share, mask, piece, low, high):
        bits, stay, pieces, size = plans[share][k]
        first = (pieces - 1 - piece) * size
        source = receive[k][share].at[(mask - 1) * pieces + piece]
        decode_add(source, size, SHARES[share][1], low - first, high - first, work[share], first, scale)

    def forward(k, share, mask, piece):
        bits, stay, pieces, size = plans[share][k]
        first = mask * stay + (pieces - 1 - piece) * size
        out = outgoing[k][share].at[(mask - 1) * pieces + piece]
        encode(lambda j: work[share][first + j], size, SHARES[share][1], out, peak, inv)
        copy = message(k, share, mask, piece, out)
        copy.start()
        in_flight[k, share, mask, piece] = copy

    for k in range(n_stages):
        for piece in range(plans[0][k][2]):
            for share in reversed(range(n_shares)):
                bits, stay, pieces, size = plans[share][k]
                masks = range(1, 2 ** len(bits))
                for mask in masks:
                    in_flight[k, share, mask, piece].wait_recv()
                top = (pieces - piece) * size
                bottom = top - size
                leaving = []
                if k + 1 < n_stages:
                    next_bits, next_stay, next_pieces, next_size = plans[share][k + 1]
                    for mask in reversed(range(1, 2 ** len(next_bits))):
                        for next_piece in range(next_pieces):
                            low = mask * next_stay + (next_pieces - 1 - next_piece) * next_size
                            if bottom <= low < top:
                                leaving.append((low, low + next_size, mask, next_piece))
                for low, high, mask, next_piece in leaving:
                    for m in masks:
                        absorb(k, share, m, piece, low, high)
                    forward(k + 1, share, mask, next_piece)
                rest = min([low for low, *_ in leaving] + [top])
                if rest > bottom:
                    for m in masks:
                        absorb(k, share, m, piece, bottom, rest)

    for share, (start, length) in enumerate(SHARES):
        total = work[share][0] + own_ref[start : start + length, :]
        work[share][0] = jnp.maximum(total, 0.0)
    hid_own[...] = jnp.concatenate([work[share][0] for share in range(n_shares)], axis=0).astype(jnp.bfloat16)

    def to_pair(src, dst, number):
        return pltpu.make_async_remote_copy(
            src_ref=src,
            dst_ref=dst,
            send_sem=pair_sem.at[0, number],
            recv_sem=pair_sem.at[1, number],
            device_id={"feat": 1 - f},
            device_id_type=MESH,
        )

    share_hidden = to_pair(hid_own, hid_other, 0)
    share_hidden.start()
    share_hidden.wait()
    mine, theirs = hid_own[...], hid_other[...]
    hidden = jnp.concatenate([jnp.where(f == 0, mine, theirs), jnp.where(f == 0, theirs, mine)], axis=0)
    width = hidden.shape[1] // 2
    def to_receiver(i):
        return pltpu.make_async_remote_copy(
            src_ref=rows_out.at[i],
            dst_ref=rows_in.at[me],
            send_sem=rows_sem.at[0],
            recv_sem=rows_sem.at[1],
            device_id={"dom": receivers[i]},
            device_id_type=MESH,
        )

    near = nx * ny
    for first in list(range(near, len(receivers), near)) + [0]:
        picked = jnp.dot(
            onehot[first * slots : (first + near) * slots, :], hidden, preferred_element_type=jnp.float32
        )
        for i in range(first, first + near):
            block = picked[(i - first) * slots : (i - first + 1) * slots, :]
            rows_out[i] = jnp.concatenate([block[:, :width], block[:, width:]], axis=0).astype(jnp.bfloat16)
        for i in range(max(first, 1), first + near):
            to_receiver(i).start()

    @pl.when(f == 0)
    def _():
        rows_in[me] = rows_out[0]

    @pl.when(f == 1)
    def _():
        to_receiver(0).start()

    n_own = hidden.shape[0]
    out_rows = out_ref.shape[0]
    own_total = jnp.dot(adj_ref[:, :n_own], hidden, preferred_element_type=jnp.float32)
    self_logits = lax.dot_general(
        hidden[:out_rows], w_self_ref[...], (((1,), (1,)), ((), ())), preferred_element_type=jnp.float32
    )
    blocks = len(receivers)

    def wait_rows(n):
        for number, ref in ((0, rows_out), (1, rows_in)):
            pltpu.make_async_copy(ref.at[pl.ds(0, n)], ref.at[pl.ds(0, n)], rows_sem.at[number]).wait()

    pl.when(f == 0)(lambda: wait_rows(blocks - 1))
    pl.when(f == 1)(lambda: wait_rows(blocks))

    arrived = rows_in[...].astype(jnp.float32)
    pool = [
        arrived[:, k * slots : (k + 1) * slots, :].reshape(parts * slots, width).astype(jnp.bfloat16)
        for k in range(2)
    ]
    for k in range(2):
        part[:, k * width : (k + 1) * width] = jnp.dot(
            adj_ref[:, n_own:], pool[k], preferred_element_type=jnp.float32
        )
    share_part = to_pair(part, part_other, 1)
    share_part.start()
    share_part.wait()
    aggregate = (part[...] + part_other[...] + own_total).astype(jnp.bfloat16)
    out_ref[...] = self_logits + lax.dot_general(
        aggregate, w_neigh_ref[...], (((1,), (1,)), ((), ())), preferred_element_type=jnp.float32
    )
    for copy in in_flight.values():
        copy.wait_send()


def second_layer(parts, keeps, messages, own, lists, counts, adj, w_self, w_neigh):
    plans = [plan_of(parts, share) for share in range(len(SHARES))]
    n_stages = len(plans[0])
    whole = pl.BlockSpec(memory_space=pltpu.VMEM)
    anywhere = pl.BlockSpec(memory_space=pl.ANY)
    rows, width = own.shape
    half = width // 2
    lengths = [length for _, length in SHARES]
    slots = lists.shape[1]
    buffers = [pltpu.VMEM((parts // 2,) + a.shape[1:], jnp.float32) for a in keeps]
    for first_stage in (0, 1):
        for k in range(first_stage, n_stages):
            for share, n in enumerate(lengths):
                bits, stay, pieces, size = plans[share][k]
                buffers.append(pltpu.VMEM(((2 ** len(bits) - 1) * pieces, size * n + size, half), jnp.int32))
    chunk = max(chunk_of(parts), 8)
    buffers += [pltpu.VMEM((chunk, half), jnp.float32)] * 3
    buffers += [
        pltpu.VMEM(lists.shape[1:], jnp.int32),
        pltpu.VMEM((parts // 2 * slots, 2 * rows), jnp.bfloat16),
        pltpu.VMEM((rows, width), jnp.bfloat16),
        pltpu.VMEM((rows, width), jnp.bfloat16),
        pltpu.VMEM((parts // 2, 2 * slots, half), jnp.bfloat16),
        pltpu.VMEM((parts, 2 * slots, half), jnp.bfloat16),
        pltpu.VMEM((adj.shape[0], width), jnp.float32),
        pltpu.VMEM((adj.shape[0], width), jnp.float32),
        pltpu.VMEM(counts.shape, counts.dtype),
        pltpu.VMEM(adj.shape, adj.dtype),
        pltpu.VMEM(w_self.shape, w_self.dtype),
        pltpu.VMEM(w_neigh.shape, w_neigh.dtype),
    ]
    numbers = max(sum((2 ** len(p[0]) - 1) * p[2] for p in plan) for plan in plans)
    dma = pltpu.SemaphoreType.DMA
    buffers += [
        dma((len(SHARES) + 5,)),
        dma((len(SHARES), numbers)),
        dma((len(SHARES), numbers)),
        dma((2, 2)),
        dma((2,)),
    ]
    return pl.pallas_call(
        functools.partial(second_layer_kernel, parts),
        out_shape=jax.ShapeDtypeStruct((adj.shape[0], w_self.shape[0]), jnp.float32),
        in_specs=[whole] * 7 + [anywhere] * 5,
        out_specs=whole,
        scratch_shapes=buffers,
        compiler_params=pltpu.CompilerParams(
            collective_id=1, has_side_effects=True, vmem_limit_bytes=SECOND_VMEM
        ),
        name="reduce_and_second_layer",
    )(*keeps, *messages, own, lists, counts, adj, w_self, w_neigh)


def body(
    features,
    tile_weight,
    tile_dst,
    tile_src,
    tile_rows,
    w_self1,
    neighbour_weight_first,
    send_list,
    send_count,
    adj_two,
    w_self2,
    w_neigh2,
):
    parts = lax.axis_size("dom")
    other, wn_other, ws_other = swap(features, neighbour_weight_first, w_self1)
    results = first_layer(
        parts,
        tile_dst,
        tile_src,
        tile_rows,
        features,
        other,
        neighbour_weight_first,
        wn_other,
        w_self1,
        ws_other,
        tile_weight,
    )
    return second_layer(parts, results[:3], results[3:6], results[6], send_list.transpose(0, 2, 1), send_count, adj_two, w_self2.T, w_neigh2.T)


def solution(mesh):
    in_specs = (
        P("dom", "feat"),
        P("dom", None, None),
        P("dom"),
        P("dom"),
        P("dom"),
        P("feat", None),
        P("feat", None),
        P(),
        P(),
        P("dom", None),
        P(),
        P(),
    )
    out_specs = P("dom", None)
    return jax.shard_map(body, mesh=mesh, in_specs=in_specs, out_specs=out_specs, check_vma=False)
```

```python
import functools

import jax
import jax.numpy as jnp
import numpy as np
from jax import lax
from jax.experimental import pallas as pl
from jax.experimental.pallas import tpu as pltpu
from jax.sharding import PartitionSpec as P

DIMS = {128: (4, 4, 8), 16: (4, 2, 2)}
SHARES = ((0, 24), (24, 24), (48, 16))


def stages_of(parts, share):
    bits = [[(axis, i) for i in range(bits_of(n))] for axis, n in enumerate(DIMS[parts])]
    x, y, z = bits
    if share == 0:
        return [x[:1], x[1:], y + z[:1], z[1:]] if len(z) > 1 else [x[:1], x[1:], y, z]
    if share == 1:
        return [y[:1], y[1:], x + z[:1], z[1:]] if len(y) > 1 else [y, x[:1], x[1:], z]
    return [z[:1], z[1:2], x[:1] + y[:1], x[1:] + y[1:] + z[2:]] if len(z) > 1 else [z, x[:1], x[1:], y]


GROUP = 4
GROUPS = 2
FIRST_VMEM = 52 * 1024 * 1024
SECOND_VMEM = 32 * 1024 * 1024
MESH = pl.DeviceIdType.MESH


def bits_of(count):
    return count.bit_length() - 1


def steps_of(parts, share):
    return [bit for stage in stages_of(parts, share) for bit in stage]


def chunk_of(parts):
    return parts // 8


def plan_of(parts, share):
    plan = []
    count = parts
    for bits in stages_of(parts, share):
        stay = count >> len(bits)
        size = min(stay, chunk_of(parts))
        plan.append((bits, stay, stay // size, size))
        count = stay
    return plan


@functools.lru_cache(maxsize=None)
def slot_table(parts):
    nx, ny, nz = DIMS[parts]
    table = np.zeros((2, len(SHARES), parts), np.int32)
    for f in range(2):
        for share in range(len(SHARES)):
            for b in range(parts):
                coords = (b % nx, b // nx % ny, b // (nx * ny))
                slot = 0
                for axis, i in steps_of(parts, share):
                    n = DIMS[parts][axis]
                    c = (coords[axis] - f) % n
                    slot = slot * 2 + ((c ^ (c >> 1)) >> i & 1)
                table[f, share, b] = slot
    return table


def place_of(parts, me):
    nx, ny, nz = DIMS[parts]
    return lax.rem(me, nx), lax.rem(lax.div(me, nx), ny), lax.div(me, nx * ny)


def chip_across(parts, me, f, bits):
    nx, ny, nz = DIMS[parts]
    place = place_of(parts, me)
    pitch = (1, nx, nx * ny)
    dom = me
    for axis, n in enumerate(DIMS[parts]):
        flips = sorted(i for a, i in bits if a == axis)
        if not flips:
            continue
        c = lax.rem(place[axis] - f + n, n)
        for i in flips:
            size = 2 ** (i + 1)
            c = c + (size - 1) - 2 * lax.rem(c, size)
        dom = dom + (lax.rem(c + f, n) - place[axis]) * pitch[axis]
    return dom


def swap_kernel(x_ref, wn_ref, ws_ref, xo_ref, wno_ref, wso_ref, send, recv):
    other = 1 - lax.axis_index("feat")
    barrier = pltpu.get_barrier_semaphore()
    pl.semaphore_signal(barrier, inc=1, device_id={"feat": other}, device_id_type=MESH)
    pl.semaphore_wait(barrier, 1)
    copies = []
    for k, (a, b) in enumerate(((x_ref, xo_ref), (wn_ref, wno_ref), (ws_ref, wso_ref))):
        copy = pltpu.make_async_remote_copy(
            src_ref=a,
            dst_ref=b,
            send_sem=send.at[k],
            recv_sem=recv.at[k],
            device_id={"feat": other},
            device_id_type=MESH,
        )
        copy.start()
        copies.append(copy)
    for copy in copies:
        copy.wait()


def swap(features, wn, ws):
    anywhere = pl.BlockSpec(memory_space=pl.ANY)
    return pl.pallas_call(
        swap_kernel,
        out_shape=[jax.ShapeDtypeStruct(a.shape, a.dtype) for a in (features, wn, ws)],
        in_specs=[anywhere] * 3,
        out_specs=[anywhere] * 3,
        scratch_shapes=[pltpu.SemaphoreType.DMA((3,)), pltpu.SemaphoreType.DMA((3,))],
        compiler_params=pltpu.CompilerParams(collective_id=0, has_side_effects=True),
        name="swap_halves",
    )(features, wn, ws)


def encode(load, count, rows, out, peak, inv):
    def largest(j, carry):
        v = jnp.abs(load(j))
        half = v.shape[1] // 2
        peak[pl.ds(j, 1), :] = jnp.max(jnp.maximum(v[:, :half], v[:, half:]), axis=0, keepdims=True)
        return carry

    lax.fori_loop(0, count, largest, 0, unroll=True)
    top = jnp.maximum(peak[:count, :], 1e-30)
    code = jnp.ceil(jnp.log2(top) * 256.0) + 1.0
    out[count * rows : count * rows + count, :] = code.astype(jnp.int32)
    inv[:count, :] = jnp.exp2(code * (-1.0 / 256.0)) * 32767.0

    def pack(j, carry):
        v = load(j)
        half = v.shape[1] // 2
        s = inv[pl.ds(j, 1), :]
        low = jnp.round(v[:, :half] * s).astype(jnp.int32)
        high = jnp.round(v[:, half:] * s).astype(jnp.int32)
        out[pl.ds(j * rows, rows), :] = jnp.bitwise_or(
            jnp.left_shift(high, 16), jnp.bitwise_and(low, 0xFFFF)
        )
        return carry

    lax.fori_loop(0, count, pack, 0, unroll=True)


def decode_add(src, total, rows, low, high, work, first, scale):
    count = high - low
    code = src[total * rows : total * rows + total, :].astype(jnp.float32)
    scale[:total, :] = jnp.exp2(code * (1.0 / 256.0)) * (1.0 / 32767.0)

    def add(j, carry):
        word = src[pl.ds((low + j) * rows, rows), :]
        s = scale[pl.ds(low + j, 1), :]
        a = jnp.right_shift(jnp.left_shift(word, 16), 16).astype(jnp.float32) * s
        b = jnp.right_shift(word, 16).astype(jnp.float32) * s
        half = a.shape[1]
        work[first + low + j, :, :half] += a
        work[first + low + j, :, half:] += b
        return carry

    lax.fori_loop(0, count, add, 0, unroll=True)


def first_layer_kernel(parts, *refs):
    table, dst, src, limit = refs[:4]
    inputs = refs[4:11]
    accs, own = refs[11:14], refs[14]
    held = refs[15:22]
    order, count, plan, gathered, load_sem = refs[22:]
    xa, xb, wa, wb, sa, sb, tiles = held
    f, me = lax.axis_index("feat"), lax.axis_index("dom")
    n_tiles, rows, size = tiles.shape
    blocks = xa.shape[0] // size
    half = parts // 2
    depth = xa.shape[1]
    group_rows = GROUP * rows

    loads = []
    for k in range(7):
        source = inputs[k].at[:, pl.ds(pl.multiple_of(f * rows, rows), rows), :] if k == 6 else inputs[k]
        copy = pltpu.make_async_copy(source, held[k], load_sem.at[k])
        copy.start()
        loads.append(copy)

    for s in range(blocks):
        count[s] = 0

    def place(t, carry):
        s = src[t]
        at = count[s]
        order[s, at] = t
        count[s] = at + 1
        clear(t)
        return carry

    def clear(j):
        for acc in accs:
            acc[j] = jnp.zeros(acc.shape[1:], jnp.float32)

    lax.fori_loop(0, n_tiles, place, 0)
    for j in range(n_tiles, parts):
        clear(j)

    def groups_of(s, at):
        n = count[s]

        def one(g, at):
            plan[0, at] = s
            plan[1, at] = g * GROUP
            plan[2, at] = jnp.minimum(n - g * GROUP, GROUP)
            return at + 1

        return lax.fori_loop(0, lax.div(n + GROUP - 1, GROUP), one, at)

    n_groups = lax.fori_loop(0, blocks, groups_of, 0)
    for g in range(3 * GROUPS):
        plan[0, n_groups + g] = 0
        plan[1, n_groups + g] = 0
        plan[2, n_groups + g] = 0

    for copy in loads:
        copy.wait()

    mine = pl.ds(pl.multiple_of(f * rows, rows), rows)
    own[...] = jnp.dot(xa[mine, :], sa[...], preferred_element_type=jnp.float32) + jnp.dot(
        xb[mine, :], sb[...], preferred_element_type=jnp.float32
    )
    row_ids = lax.broadcasted_iota(jnp.int32, (rows, size), 0) + f * rows
    bases = [table[f, share, me] for share in range(len(SHARES))]

    def gather(g, buffer):
        for u in range(GROUPS):
            s, first, n = plan[0, g + u], plan[1, g + u], plan[2, g + u]
            pieces = []
            for j in range(GROUP):
                valid = j < n
                t = jnp.where(valid, order[s, first + j], 0)
                tile = tiles[t]
                pieces.append(jnp.where(row_ids < jnp.where(valid, limit[t], 0), tile, jnp.zeros_like(tile)))
            a = jnp.concatenate(pieces, axis=0)
            at_source = pl.ds(pl.multiple_of(s * size, size), size)
            at = slice(u * group_rows, (u + 1) * group_rows)
            buffer[at, :depth] = jnp.dot(a, xa[at_source, :], preferred_element_type=jnp.float32).astype(
                jnp.bfloat16
            )
            buffer[at, depth:] = jnp.dot(a, xb[at_source, :], preferred_element_type=jnp.float32).astype(
                jnp.bfloat16
            )

    def spread(g, buffer):
        h = jnp.dot(buffer[:, :depth], wa[...], preferred_element_type=jnp.float32) + jnp.dot(
            buffer[:, depth:], wb[...], preferred_element_type=jnp.float32
        )
        for u in range(GROUPS):
            s, first, n = plan[0, g + u], plan[1, g + u], plan[2, g + u]
            for j in range(GROUP):
                d = dst[jnp.where(j < n, order[s, first + j], 0)]
                for share, (start, length) in enumerate(SHARES):
                    slot = jnp.bitwise_xor(table[f, share, d], bases[share])
                    at = (u * GROUP + j) * rows + start
                    accs[share][slot] += h[at : at + length, :]

    gather(0, gathered.at[0])

    def step(i, carry):
        g = i * (2 * GROUPS)
        spread(g, gathered.at[0])
        gather(g + GROUPS, gathered.at[1])
        spread(g + GROUPS, gathered.at[1])
        gather(g + 2 * GROUPS, gathered.at[0])
        return carry

    lax.fori_loop(0, lax.div(n_groups + 2 * GROUPS - 1, 2 * GROUPS), step, 0)


def first_layer(parts, dst, src, limit, features, other, wn, wn_other, ws, ws_other, tiles):
    n_tiles, size, _ = tiles.shape
    rows = size // 2
    width = wn.shape[1]
    scalars = pl.BlockSpec(memory_space=pltpu.SMEM)
    anywhere = pl.BlockSpec(memory_space=pl.ANY)
    lengths = [length for _, length in SHARES]
    operands = (features, other, wn, wn_other, ws, ws_other)
    blocks = features.shape[0] // size
    return pl.pallas_call(
        functools.partial(first_layer_kernel, parts),
        in_specs=[scalars] * 4 + [anywhere] * 7,
        out_specs=[pl.BlockSpec(memory_space=pltpu.VMEM)] * 4,
        scratch_shapes=[pltpu.VMEM(a.shape, a.dtype) for a in operands]
        + [
            pltpu.VMEM((n_tiles, rows, size), tiles.dtype),
            pltpu.SMEM((blocks, n_tiles + GROUP), jnp.int32),
            pltpu.SMEM((blocks,), jnp.int32),
            pltpu.SMEM((3, n_tiles // GROUP + blocks + 3 * GROUPS), jnp.int32),
            pltpu.VMEM((2, GROUPS * GROUP * rows, 2 * features.shape[1]), jnp.bfloat16),
            pltpu.SemaphoreType.DMA((7,)),
        ],
        out_shape=[pltpu.VMEM((parts, n, width), jnp.float32) for n in lengths]
        + [pltpu.VMEM((rows, width), jnp.float32)],
        compiler_params=pltpu.CompilerParams(vmem_limit_bytes=FIRST_VMEM),
        name="first_layer",
    )(jnp.asarray(slot_table(parts)), dst, src, limit, *operands, tiles)


def second_layer_kernel(parts, *refs):
    nx, ny, nz = DIMS[parts]
    plane = nx * ny
    n_shares = len(SHARES)
    plans = [plan_of(parts, share) for share in range(n_shares)]
    n_stages = len(plans[0])
    keeps = refs[0:3]
    own_ref, list_ref, count_hbm, adj_hbm, w_self_hbm, w_neigh_hbm, out_ref = refs[3:10]
    work, messages = refs[10:13], refs[13:16]
    at = 16
    receive, outgoing = [], []
    for k in range(n_stages):
        receive.append(refs[at : at + 3])
        at += 3
    for k in range(n_stages):
        outgoing.append(refs[at : at + 3] if k > 0 else None)
        at += 3 if k > 0 else 0
    (peak, inv, scale, lists, onehot, hid_own, hid_other, rows_out, rows_in, part, part_other) = refs[at : at + 11]
    count_ref, adj_ref, w_self_ref, w_neigh_ref = refs[at + 11 : at + 15]
    local_sem, send_sem, recv_sem, pair_sem, rows_sem = refs[at + 15 :]

    f = lax.axis_index("feat")
    me = lax.axis_index("dom")
    partners = {}
    for share in range(n_shares):
        for k, (bits, stay, pieces, size) in enumerate(plans[share]):
            for mask in range(1, 2 ** len(bits)):
                chosen = tuple(sorted(b for i, b in enumerate(bits) if mask >> (len(bits) - 1 - i) & 1))
                if chosen not in partners:
                    partners[chosen] = chip_across(parts, me, f, chosen)
    barrier = pltpu.get_barrier_semaphore()
    for target in [{"feat": 1 - f}] + [{"dom": dom} for dom in partners.values()]:
        pl.semaphore_signal(barrier, inc=1, device_id=target, device_id_type=MESH)
    rows_in[...] = jnp.zeros_like(rows_in)

    def encode_first(piece):
        for share, (_, length) in enumerate(SHARES):
            bits, stay, pieces, size = plans[share][0]
            first = stay + (pieces - 1 - piece) * size
            keep = keeps[share]
            encode(lambda j: keep[first + j], size, length, messages[share].at[piece], peak, inv)

    encode_first(0)
    pl.semaphore_wait(barrier, 1 + len(partners))

    def message(k, share, mask, piece, src):
        bits, stay, pieces, size = plans[share][k]
        index = (mask - 1) * pieces + piece
        number = sum((2 ** len(p[0]) - 1) * p[2] for p in plans[share][:k]) + index
        chosen = tuple(sorted(b for i, b in enumerate(bits) if mask >> (len(bits) - 1 - i) & 1))
        return pltpu.make_async_remote_copy(
            src_ref=src,
            dst_ref=receive[k][share].at[index],
            send_sem=send_sem.at[share, number],
            recv_sem=recv_sem.at[share, number],
            device_id={"dom": partners[chosen]},
            device_id_type=MESH,
        )

    in_flight = {}
    for piece in range(plans[0][0][2]):
        if piece > 0:
            encode_first(piece)
        for share in range(n_shares):
            copy = message(0, share, 1, piece, messages[share].at[piece])
            copy.start()
            in_flight[0, share, 1, piece] = copy
    loads = []
    for share in range(n_shares):
        copy = pltpu.make_async_copy(keeps[share].at[pl.ds(0, parts // 2)], work[share], local_sem.at[share])
        copy.start()
        loads.append(copy)

    get_lists = pltpu.make_async_copy(list_ref.at[me], lists, local_sem.at[len(SHARES)])
    get_lists.start()
    loads.append(get_lists)
    late = ((count_hbm, count_ref), (adj_hbm, adj_ref), (w_self_hbm, w_self_ref), (w_neigh_hbm, w_neigh_ref))
    for k, (source, target) in enumerate(late):
        copy = pltpu.make_async_copy(source, target, local_sem.at[len(SHARES) + 1 + k])
        copy.start()
        loads.append(copy)
    for copy in loads:
        copy.wait()
    slots = lists.shape[0]
    shape = lists.shape
    lanes = lax.broadcasted_iota(jnp.int32, shape, 1)
    valid = lax.broadcasted_iota(jnp.int32, shape, 0) < count_ref[pl.ds(me, 1), :]
    wanted = jnp.where(valid, lists[...], -1).astype(jnp.float32)
    hidden_rows = onehot.shape[1]
    ids = lax.broadcasted_iota(jnp.int32, (slots, hidden_rows), 1).astype(jnp.float32)
    px, py, pz = place_of(parts, me)
    at_x = [lax.rem(px + d, nx) for d in range(nx)]
    at_y = [lax.rem(py + d, ny) * nx for d in range(ny)]
    at_z = [lax.rem(pz + d, nz) * (nx * ny) for d in range(nz)]
    receivers = []
    for d in [0] + sorted(range(1, nz // 2), key=lambda d: -min(2 * d, nz - 2 * d)):
        by_parity = [jnp.where(f == odd, at_z[2 * d], at_z[2 * d + 1]) for odd in range(2)]
        for dy in range(ny):
            for dx in range(nx):
                receivers.append(at_x[dx] + at_y[dy] + by_parity[(dx + dy) % 2])

    for i in range(0, len(receivers), 2):
        pair = []
        for r in receivers[i : i + 2]:
            column = jnp.sum(jnp.where(lanes == r, wanted, 0.0), axis=1, keepdims=True)
            pair.append(jnp.where(column == ids, 1.0, 0.0))
        onehot[i * slots : (i + 2) * slots, :] = jnp.concatenate(pair, axis=0).astype(jnp.bfloat16)

    def absorb(k, share, mask, piece, low, high):
        bits, stay, pieces, size = plans[share][k]
        first = (pieces - 1 - piece) * size
        source = receive[k][share].at[(mask - 1) * pieces + piece]
        decode_add(source, size, SHARES[share][1], low - first, high - first, work[share], first, scale)

    def forward(k, share, mask, piece):
        bits, stay, pieces, size = plans[share][k]
        first = mask * stay + (pieces - 1 - piece) * size
        out = outgoing[k][share].at[(mask - 1) * pieces + piece]
        encode(lambda j: work[share][first + j], size, SHARES[share][1], out, peak, inv)
        copy = message(k, share, mask, piece, out)
        copy.start()
        in_flight[k, share, mask, piece] = copy

    for k in range(n_stages):
        for piece in range(plans[0][k][2]):
            for share in reversed(range(n_shares)):
                bits, stay, pieces, size = plans[share][k]
                masks = range(1, 2 ** len(bits))
                for mask in masks:
                    in_flight[k, share, mask, piece].wait_recv()
                top = (pieces - piece) * size
                bottom = top - size
                leaving = []
                if k + 1 < n_stages:
                    next_bits, next_stay, next_pieces, next_size = plans[share][k + 1]
                    for mask in reversed(range(1, 2 ** len(next_bits))):
                        for next_piece in range(next_pieces):
                            low = mask * next_stay + (next_pieces - 1 - next_piece) * next_size
                            if bottom <= low < top:
                                leaving.append((low, low + next_size, mask, next_piece))
                for low, high, mask, next_piece in leaving:
                    for m in masks:
                        absorb(k, share, m, piece, low, high)
                    forward(k + 1, share, mask, next_piece)
                rest = min([low for low, *_ in leaving] + [top])
                if rest > bottom:
                    for m in masks:
                        absorb(k, share, m, piece, bottom, rest)

    for share, (start, length) in enumerate(SHARES):
        total = work[share][0] + own_ref[start : start + length, :]
        work[share][0] = jnp.maximum(total, 0.0)
    hid_own[...] = jnp.concatenate([work[share][0] for share in range(n_shares)], axis=0).astype(jnp.bfloat16)

    def to_pair(src, dst, number):
        return pltpu.make_async_remote_copy(
            src_ref=src,
            dst_ref=dst,
            send_sem=pair_sem.at[0, number],
            recv_sem=pair_sem.at[1, number],
            device_id={"feat": 1 - f},
            device_id_type=MESH,
        )

    share_hidden = to_pair(hid_own, hid_other, 0)
    share_hidden.start()
    share_hidden.wait()
    mine, theirs = hid_own[...], hid_other[...]
    hidden = jnp.concatenate([jnp.where(f == 0, mine, theirs), jnp.where(f == 0, theirs, mine)], axis=0)
    width = hidden.shape[1] // 2
    def to_receiver(i):
        return pltpu.make_async_remote_copy(
            src_ref=rows_out.at[i],
            dst_ref=rows_in.at[me],
            send_sem=rows_sem.at[0],
            recv_sem=rows_sem.at[1],
            device_id={"dom": receivers[i]},
            device_id_type=MESH,
        )

    near = nx * ny
    for first in list(range(near, len(receivers), near)) + [0]:
        picked = jnp.dot(
            onehot[first * slots : (first + near) * slots, :], hidden, preferred_element_type=jnp.float32
        )
        for i in range(first, first + near):
            block = picked[(i - first) * slots : (i - first + 1) * slots, :]
            rows_out[i] = jnp.concatenate([block[:, :width], block[:, width:]], axis=0).astype(jnp.bfloat16)
        for i in range(max(first, 1), first + near):
            to_receiver(i).start()

    @pl.when(f == 0)
    def _():
        rows_in[me] = rows_out[0]

    @pl.when(f == 1)
    def _():
        to_receiver(0).start()

    n_own = hidden.shape[0]
    out_rows = out_ref.shape[0]
    own_total = jnp.dot(adj_ref[:, :n_own], hidden, preferred_element_type=jnp.float32)
    self_logits = lax.dot_general(
        hidden[:out_rows], w_self_ref[...], (((1,), (1,)), ((), ())), preferred_element_type=jnp.float32
    )
    blocks = len(receivers)

    def wait_rows(n):
        for number, ref in ((0, rows_out), (1, rows_in)):
            pltpu.make_async_copy(ref.at[pl.ds(0, n)], ref.at[pl.ds(0, n)], rows_sem.at[number]).wait()

    pl.when(f == 0)(lambda: wait_rows(blocks - 1))
    pl.when(f == 1)(lambda: wait_rows(blocks))

    arrived = rows_in[...].astype(jnp.float32)
    pool = [
        arrived[:, k * slots : (k + 1) * slots, :].reshape(parts * slots, width).astype(jnp.bfloat16)
        for k in range(2)
    ]
    for k in range(2):
        part[:, k * width : (k + 1) * width] = jnp.dot(
            adj_ref[:, n_own:], pool[k], preferred_element_type=jnp.float32
        )
    share_part = to_pair(part, part_other, 1)
    share_part.start()
    share_part.wait()
    aggregate = (part[...] + part_other[...] + own_total).astype(jnp.bfloat16)
    out_ref[...] = self_logits + lax.dot_general(
        aggregate, w_neigh_ref[...], (((1,), (1,)), ((), ())), preferred_element_type=jnp.float32
    )
    for copy in in_flight.values():
        copy.wait_send()


def second_layer(parts, keeps, own, lists, counts, adj, w_self, w_neigh):
    plans = [plan_of(parts, share) for share in range(len(SHARES))]
    n_stages = len(plans[0])
    whole = pl.BlockSpec(memory_space=pltpu.VMEM)
    anywhere = pl.BlockSpec(memory_space=pl.ANY)
    rows, width = own.shape
    half = width // 2
    lengths = [length for _, length in SHARES]
    slots = lists.shape[1]
    buffers = [pltpu.VMEM((parts // 2,) + a.shape[1:], jnp.float32) for a in keeps]
    for first_stage in (None, 0, 1):
        for k in range(1) if first_stage is None else range(first_stage, n_stages):
            for share, n in enumerate(lengths):
                bits, stay, pieces, size = plans[share][k]
                buffers.append(pltpu.VMEM(((2 ** len(bits) - 1) * pieces, size * n + size, half), jnp.int32))
    chunk = max(chunk_of(parts), 8)
    buffers += [pltpu.VMEM((chunk, half), jnp.float32)] * 3
    buffers += [
        pltpu.VMEM(lists.shape[1:], jnp.int32),
        pltpu.VMEM((parts // 2 * slots, 2 * rows), jnp.bfloat16),
        pltpu.VMEM((rows, width), jnp.bfloat16),
        pltpu.VMEM((rows, width), jnp.bfloat16),
        pltpu.VMEM((parts // 2, 2 * slots, half), jnp.bfloat16),
        pltpu.VMEM((parts, 2 * slots, half), jnp.bfloat16),
        pltpu.VMEM((adj.shape[0], width), jnp.float32),
        pltpu.VMEM((adj.shape[0], width), jnp.float32),
        pltpu.VMEM(counts.shape, counts.dtype),
        pltpu.VMEM(adj.shape, adj.dtype),
        pltpu.VMEM(w_self.shape, w_self.dtype),
        pltpu.VMEM(w_neigh.shape, w_neigh.dtype),
    ]
    numbers = max(sum((2 ** len(p[0]) - 1) * p[2] for p in plan) for plan in plans)
    dma = pltpu.SemaphoreType.DMA
    buffers += [
        dma((len(SHARES) + 5,)),
        dma((len(SHARES), numbers)),
        dma((len(SHARES), numbers)),
        dma((2, 2)),
        dma((2,)),
    ]
    return pl.pallas_call(
        functools.partial(second_layer_kernel, parts),
        out_shape=jax.ShapeDtypeStruct((adj.shape[0], w_self.shape[0]), jnp.float32),
        in_specs=[whole] * 4 + [anywhere] * 5,
        out_specs=whole,
        scratch_shapes=buffers,
        compiler_params=pltpu.CompilerParams(
            collective_id=1, has_side_effects=True, vmem_limit_bytes=SECOND_VMEM
        ),
        name="reduce_and_second_layer",
    )(*keeps, own, lists, counts, adj, w_self, w_neigh)


def body(
    features,
    tile_weight,
    tile_dst,
    tile_src,
    tile_rows,
    w_self1,
    neighbour_weight_first,
    send_list,
    send_count,
    adj_two,
    w_self2,
    w_neigh2,
):
    parts = lax.axis_size("dom")
    other, wn_other, ws_other = swap(features, neighbour_weight_first, w_self1)
    results = first_layer(
        parts,
        tile_dst,
        tile_src,
        tile_rows,
        features,
        other,
        neighbour_weight_first,
        wn_other,
        w_self1,
        ws_other,
        tile_weight,
    )
    return second_layer(parts, results[:3], results[3], send_list.transpose(0, 2, 1), send_count, adj_two, w_self2.T, w_neigh2.T)


def solution(mesh):
    in_specs = (
        P("dom", "feat"),
        P("dom", None, None),
        P("dom"),
        P("dom"),
        P("dom"),
        P("feat", None),
        P("feat", None),
        P(),
        P(),
        P("dom", None),
        P(),
        P(),
    )
    out_specs = P("dom", None)
    return jax.shard_map(body, mesh=mesh, in_specs=in_specs, out_specs=out_specs, check_vma=False)
```

```python
import functools

import jax
import jax.numpy as jnp
import numpy as np
from jax import lax
from jax.experimental import pallas as pl
from jax.experimental.pallas import tpu as pltpu
from jax.sharding import PartitionSpec as P

DIMS = {128: (4, 4, 8), 16: (4, 2, 2)}
SHARES = ((0, 24), (24, 24), (48, 16))


def stages_of(parts, share):
    bits = [[(axis, i) for i in range(bits_of(n))] for axis, n in enumerate(DIMS[parts])]
    x, y, z = bits
    if share == 0:
        return [x[:1], x[1:], y + z[:1], z[1:]] if len(z) > 1 else [x[:1], x[1:], y, z]
    if share == 1:
        return [y[:1], y[1:], x + z[:1], z[1:]] if len(y) > 1 else [y, x[:1], x[1:], z]
    return [z[:1], z[1:2], x[:1] + y[:1], x[1:] + y[1:] + z[2:]] if len(z) > 1 else [z, x[:1], x[1:], y]


GROUP = 4
GROUPS = 2
FIRST_VMEM = 52 * 1024 * 1024
SECOND_VMEM = 32 * 1024 * 1024
MESH = pl.DeviceIdType.MESH


def bits_of(count):
    return count.bit_length() - 1


def steps_of(parts, share):
    return [bit for stage in stages_of(parts, share) for bit in stage]


def chunk_of(parts):
    return parts // 8


def plan_of(parts, share):
    plan = []
    count = parts
    for bits in stages_of(parts, share):
        stay = count >> len(bits)
        size = min(stay, chunk_of(parts))
        plan.append((bits, stay, stay // size, size))
        count = stay
    return plan


@functools.lru_cache(maxsize=None)
def slot_table(parts):
    nx, ny, nz = DIMS[parts]
    table = np.zeros((2, len(SHARES), parts), np.int32)
    for f in range(2):
        for share in range(len(SHARES)):
            for b in range(parts):
                coords = (b % nx, b // nx % ny, b // (nx * ny))
                slot = 0
                for axis, i in steps_of(parts, share):
                    n = DIMS[parts][axis]
                    c = (coords[axis] - f) % n
                    slot = slot * 2 + ((c ^ (c >> 1)) >> i & 1)
                table[f, share, b] = slot
    return table


def place_of(parts, me):
    nx, ny, nz = DIMS[parts]
    return lax.rem(me, nx), lax.rem(lax.div(me, nx), ny), lax.div(me, nx * ny)


def chip_across(parts, me, f, bits):
    nx, ny, nz = DIMS[parts]
    place = place_of(parts, me)
    pitch = (1, nx, nx * ny)
    dom = me
    for axis, n in enumerate(DIMS[parts]):
        flips = sorted(i for a, i in bits if a == axis)
        if not flips:
            continue
        c = lax.rem(place[axis] - f + n, n)
        for i in flips:
            size = 2 ** (i + 1)
            c = c + (size - 1) - 2 * lax.rem(c, size)
        dom = dom + (lax.rem(c + f, n) - place[axis]) * pitch[axis]
    return dom


def swap_kernel(x_ref, wn_ref, ws_ref, xo_ref, wno_ref, wso_ref, send, recv):
    other = 1 - lax.axis_index("feat")
    barrier = pltpu.get_barrier_semaphore()
    pl.semaphore_signal(barrier, inc=1, device_id={"feat": other}, device_id_type=MESH)
    pl.semaphore_wait(barrier, 1)
    copies = []
    for k, (a, b) in enumerate(((x_ref, xo_ref), (wn_ref, wno_ref), (ws_ref, wso_ref))):
        copy = pltpu.make_async_remote_copy(
            src_ref=a,
            dst_ref=b,
            send_sem=send.at[k],
            recv_sem=recv.at[k],
            device_id={"feat": other},
            device_id_type=MESH,
        )
        copy.start()
        copies.append(copy)
    for copy in copies:
        copy.wait()


def swap(features, wn, ws):
    anywhere = pl.BlockSpec(memory_space=pl.ANY)
    return pl.pallas_call(
        swap_kernel,
        out_shape=[jax.ShapeDtypeStruct(a.shape, a.dtype) for a in (features, wn, ws)],
        in_specs=[anywhere] * 3,
        out_specs=[anywhere] * 3,
        scratch_shapes=[pltpu.SemaphoreType.DMA((3,)), pltpu.SemaphoreType.DMA((3,))],
        compiler_params=pltpu.CompilerParams(collective_id=0, has_side_effects=True),
        name="swap_halves",
    )(features, wn, ws)


def encode(load, count, rows, out, peak, inv):
    def largest(j, carry):
        v = jnp.abs(load(j))
        half = v.shape[1] // 2
        peak[pl.ds(j, 1), :] = jnp.max(jnp.maximum(v[:, :half], v[:, half:]), axis=0, keepdims=True)
        return carry

    lax.fori_loop(0, count, largest, 0, unroll=True)
    top = jnp.maximum(peak[:count, :], 1e-30)
    code = jnp.ceil(jnp.log2(top) * 256.0) + 1.0
    out[count * rows : count * rows + count, :] = code.astype(jnp.int32)
    inv[:count, :] = jnp.exp2(code * (-1.0 / 256.0)) * 32767.0

    def pack(j, carry):
        v = load(j)
        half = v.shape[1] // 2
        s = inv[pl.ds(j, 1), :]
        low = jnp.round(v[:, :half] * s).astype(jnp.int32)
        high = jnp.round(v[:, half:] * s).astype(jnp.int32)
        out[pl.ds(j * rows, rows), :] = jnp.bitwise_or(
            jnp.left_shift(high, 16), jnp.bitwise_and(low, 0xFFFF)
        )
        return carry

    lax.fori_loop(0, count, pack, 0, unroll=True)


def decode_add(src, total, rows, low, high, work, first, scale):
    count = high - low
    code = src[total * rows : total * rows + total, :].astype(jnp.float32)
    scale[:total, :] = jnp.exp2(code * (1.0 / 256.0)) * (1.0 / 32767.0)

    def add(j, carry):
        word = src[pl.ds((low + j) * rows, rows), :]
        s = scale[pl.ds(low + j, 1), :]
        a = jnp.right_shift(jnp.left_shift(word, 16), 16).astype(jnp.float32) * s
        b = jnp.right_shift(word, 16).astype(jnp.float32) * s
        half = a.shape[1]
        work[first + low + j, :, :half] += a
        work[first + low + j, :, half:] += b
        return carry

    lax.fori_loop(0, count, add, 0, unroll=True)


def first_layer_kernel(parts, *refs):
    table, dst, src, limit = refs[:4]
    inputs = refs[4:11]
    accs, own = refs[11:14], refs[14]
    held = refs[15:22]
    order, count, plan, gathered, load_sem = refs[22:]
    xa, xb, wa, wb, sa, sb, tiles = held
    f, me = lax.axis_index("feat"), lax.axis_index("dom")
    n_tiles, rows, size = tiles.shape
    blocks = xa.shape[0] // size
    half = parts // 2
    depth = xa.shape[1]
    group_rows = GROUP * rows

    loads = []
    for k in range(7):
        source = inputs[k].at[:, pl.ds(pl.multiple_of(f * rows, rows), rows), :] if k == 6 else inputs[k]
        copy = pltpu.make_async_copy(source, held[k], load_sem.at[k])
        copy.start()
        loads.append(copy)

    for s in range(blocks):
        count[s] = 0

    def place(t, carry):
        s = src[t]
        at = count[s]
        order[s, at] = t
        count[s] = at + 1
        clear(t)
        return carry

    def clear(j):
        for acc in accs:
            acc[j] = jnp.zeros(acc.shape[1:], jnp.float32)

    lax.fori_loop(0, n_tiles, place, 0, unroll=8)
    for j in range(n_tiles, parts):
        clear(j)

    def groups_of(s, at):
        n = count[s]

        def one(g, at):
            plan[0, at] = s
            plan[1, at] = g * GROUP
            plan[2, at] = jnp.minimum(n - g * GROUP, GROUP)
            return at + 1

        return lax.fori_loop(0, lax.div(n + GROUP - 1, GROUP), one, at)

    n_groups = lax.fori_loop(0, blocks, groups_of, 0)
    for g in range(3 * GROUPS):
        plan[0, n_groups + g] = 0
        plan[1, n_groups + g] = 0
        plan[2, n_groups + g] = 0

    for copy in loads:
        copy.wait()

    mine = pl.ds(pl.multiple_of(f * rows, rows), rows)
    own[...] = jnp.dot(xa[mine, :], sa[...], preferred_element_type=jnp.float32) + jnp.dot(
        xb[mine, :], sb[...], preferred_element_type=jnp.float32
    )
    row_ids = lax.broadcasted_iota(jnp.int32, (rows, size), 0) + f * rows
    bases = [table[f, share, me] for share in range(len(SHARES))]

    def gather(g, buffer):
        for u in range(GROUPS):
            s, first, n = plan[0, g + u], plan[1, g + u], plan[2, g + u]
            pieces = []
            for j in range(GROUP):
                valid = j < n
                t = jnp.where(valid, order[s, first + j], 0)
                tile = tiles[t]
                pieces.append(jnp.where(row_ids < jnp.where(valid, limit[t], 0), tile, jnp.zeros_like(tile)))
            a = jnp.concatenate(pieces, axis=0)
            at_source = pl.ds(pl.multiple_of(s * size, size), size)
            at = slice(u * group_rows, (u + 1) * group_rows)
            buffer[at, :depth] = jnp.dot(a, xa[at_source, :], preferred_element_type=jnp.float32).astype(
                jnp.bfloat16
            )
            buffer[at, depth:] = jnp.dot(a, xb[at_source, :], preferred_element_type=jnp.float32).astype(
                jnp.bfloat16
            )

    def spread(g, buffer):
        h = jnp.dot(buffer[:, :depth], wa[...], preferred_element_type=jnp.float32) + jnp.dot(
            buffer[:, depth:], wb[...], preferred_element_type=jnp.float32
        )
        for u in range(GROUPS):
            s, first, n = plan[0, g + u], plan[1, g + u], plan[2, g + u]
            for j in range(GROUP):
                d = dst[jnp.where(j < n, order[s, first + j], 0)]
                for share, (start, length) in enumerate(SHARES):
                    slot = jnp.bitwise_xor(table[f, share, d], bases[share])
                    at = (u * GROUP + j) * rows + start
                    accs[share][slot] += h[at : at + length, :]

    gather(0, gathered.at[0])

    def step(i, carry):
        g = i * (2 * GROUPS)
        spread(g, gathered.at[0])
        gather(g + GROUPS, gathered.at[1])
        spread(g + GROUPS, gathered.at[1])
        gather(g + 2 * GROUPS, gathered.at[0])
        return carry

    lax.fori_loop(0, lax.div(n_groups + 2 * GROUPS - 1, 2 * GROUPS), step, 0)


def first_layer(parts, dst, src, limit, features, other, wn, wn_other, ws, ws_other, tiles):
    n_tiles, size, _ = tiles.shape
    rows = size // 2
    width = wn.shape[1]
    scalars = pl.BlockSpec(memory_space=pltpu.SMEM)
    anywhere = pl.BlockSpec(memory_space=pl.ANY)
    lengths = [length for _, length in SHARES]
    operands = (features, other, wn, wn_other, ws, ws_other)
    blocks = features.shape[0] // size
    return pl.pallas_call(
        functools.partial(first_layer_kernel, parts),
        in_specs=[scalars] * 4 + [anywhere] * 7,
        out_specs=[pl.BlockSpec(memory_space=pltpu.VMEM)] * 4,
        scratch_shapes=[pltpu.VMEM(a.shape, a.dtype) for a in operands]
        + [
            pltpu.VMEM((n_tiles, rows, size), tiles.dtype),
            pltpu.SMEM((blocks, n_tiles + GROUP), jnp.int32),
            pltpu.SMEM((blocks,), jnp.int32),
            pltpu.SMEM((3, n_tiles // GROUP + blocks + 3 * GROUPS), jnp.int32),
            pltpu.VMEM((2, GROUPS * GROUP * rows, 2 * features.shape[1]), jnp.bfloat16),
            pltpu.SemaphoreType.DMA((7,)),
        ],
        out_shape=[pltpu.VMEM((parts, n, width), jnp.float32) for n in lengths]
        + [pltpu.VMEM((rows, width), jnp.float32)],
        compiler_params=pltpu.CompilerParams(vmem_limit_bytes=FIRST_VMEM),
        name="first_layer",
    )(jnp.asarray(slot_table(parts)), dst, src, limit, *operands, tiles)


def second_layer_kernel(parts, *refs):
    nx, ny, nz = DIMS[parts]
    plane = nx * ny
    n_shares = len(SHARES)
    plans = [plan_of(parts, share) for share in range(n_shares)]
    n_stages = len(plans[0])
    keeps = refs[0:3]
    own_ref, list_ref, count_hbm, adj_hbm, w_self_hbm, w_neigh_hbm, out_ref = refs[3:10]
    work, messages = refs[10:13], refs[13:16]
    at = 16
    receive, outgoing = [], []
    for k in range(n_stages):
        receive.append(refs[at : at + 3])
        at += 3
    for k in range(n_stages):
        outgoing.append(refs[at : at + 3] if k > 0 else None)
        at += 3 if k > 0 else 0
    (peak, inv, scale, lists, onehot, hid_own, hid_other, rows_out, rows_in, part, part_other) = refs[at : at + 11]
    count_ref, adj_ref, w_self_ref, w_neigh_ref = refs[at + 11 : at + 15]
    local_sem, send_sem, recv_sem, pair_sem, rows_sem = refs[at + 15 :]

    f = lax.axis_index("feat")
    me = lax.axis_index("dom")
    partners = {}
    for share in range(n_shares):
        for k, (bits, stay, pieces, size) in enumerate(plans[share]):
            for mask in range(1, 2 ** len(bits)):
                chosen = tuple(sorted(b for i, b in enumerate(bits) if mask >> (len(bits) - 1 - i) & 1))
                if chosen not in partners:
                    partners[chosen] = chip_across(parts, me, f, chosen)
    barrier = pltpu.get_barrier_semaphore()
    for target in [{"feat": 1 - f}] + [{"dom": dom} for dom in partners.values()]:
        pl.semaphore_signal(barrier, inc=1, device_id=target, device_id_type=MESH)
    rows_in[...] = jnp.zeros_like(rows_in)

    def encode_first(piece):
        for share, (_, length) in enumerate(SHARES):
            bits, stay, pieces, size = plans[share][0]
            first = stay + (pieces - 1 - piece) * size
            keep = keeps[share]
            encode(lambda j: keep[first + j], size, length, messages[share].at[piece], peak, inv)

    encode_first(0)
    pl.semaphore_wait(barrier, 1 + len(partners))

    def message(k, share, mask, piece, src):
        bits, stay, pieces, size = plans[share][k]
        index = (mask - 1) * pieces + piece
        number = sum((2 ** len(p[0]) - 1) * p[2] for p in plans[share][:k]) + index
        chosen = tuple(sorted(b for i, b in enumerate(bits) if mask >> (len(bits) - 1 - i) & 1))
        return pltpu.make_async_remote_copy(
            src_ref=src,
            dst_ref=receive[k][share].at[index],
            send_sem=send_sem.at[share, number],
            recv_sem=recv_sem.at[share, number],
            device_id={"dom": partners[chosen]},
            device_id_type=MESH,
        )

    in_flight = {}
    for piece in range(plans[0][0][2]):
        if piece > 0:
            encode_first(piece)
        for share in range(n_shares):
            copy = message(0, share, 1, piece, messages[share].at[piece])
            copy.start()
            in_flight[0, share, 1, piece] = copy
    loads = []
    for share in range(n_shares):
        copy = pltpu.make_async_copy(keeps[share].at[pl.ds(0, parts // 2)], work[share], local_sem.at[share])
        copy.start()
        loads.append(copy)

    get_lists = pltpu.make_async_copy(list_ref.at[me], lists, local_sem.at[len(SHARES)])
    get_lists.start()
    loads.append(get_lists)
    late = ((count_hbm, count_ref), (adj_hbm, adj_ref), (w_self_hbm, w_self_ref), (w_neigh_hbm, w_neigh_ref))
    for k, (source, target) in enumerate(late):
        copy = pltpu.make_async_copy(source, target, local_sem.at[len(SHARES) + 1 + k])
        copy.start()
        loads.append(copy)
    for copy in loads:
        copy.wait()
    slots = lists.shape[0]
    shape = lists.shape
    lanes = lax.broadcasted_iota(jnp.int32, shape, 1)
    valid = lax.broadcasted_iota(jnp.int32, shape, 0) < count_ref[pl.ds(me, 1), :]
    wanted = jnp.where(valid, lists[...], -1).astype(jnp.float32)
    hidden_rows = onehot.shape[1]
    ids = lax.broadcasted_iota(jnp.int32, (slots, hidden_rows), 1).astype(jnp.float32)
    px, py, pz = place_of(parts, me)
    at_x = [lax.rem(px + d, nx) for d in range(nx)]
    at_y = [lax.rem(py + d, ny) * nx for d in range(ny)]
    at_z = [lax.rem(pz + d, nz) * (nx * ny) for d in range(nz)]
    receivers = []
    for d in [0] + sorted(range(1, nz // 2), key=lambda d: -min(2 * d, nz - 2 * d)):
        by_parity = [jnp.where(f == odd, at_z[2 * d], at_z[2 * d + 1]) for odd in range(2)]
        for dy in range(ny):
            for dx in range(nx):
                receivers.append(at_x[dx] + at_y[dy] + by_parity[(dx + dy) % 2])

    for i in range(0, len(receivers), 2):
        pair = []
        for r in receivers[i : i + 2]:
            column = jnp.sum(jnp.where(lanes == r, wanted, 0.0), axis=1, keepdims=True)
            pair.append(jnp.where(column == ids, 1.0, 0.0))
        onehot[i * slots : (i + 2) * slots, :] = jnp.concatenate(pair, axis=0).astype(jnp.bfloat16)

    def absorb(k, share, mask, piece, low, high):
        bits, stay, pieces, size = plans[share][k]
        first = (pieces - 1 - piece) * size
        source = receive[k][share].at[(mask - 1) * pieces + piece]
        decode_add(source, size, SHARES[share][1], low - first, high - first, work[share], first, scale)

    def forward(k, share, mask, piece):
        bits, stay, pieces, size = plans[share][k]
        first = mask * stay + (pieces - 1 - piece) * size
        out = outgoing[k][share].at[(mask - 1) * pieces + piece]
        encode(lambda j: work[share][first + j], size, SHARES[share][1], out, peak, inv)
        copy = message(k, share, mask, piece, out)
        copy.start()
        in_flight[k, share, mask, piece] = copy

    for k in range(n_stages):
        for piece in range(plans[0][k][2]):
            for share in reversed(range(n_shares)):
                bits, stay, pieces, size = plans[share][k]
                masks = range(1, 2 ** len(bits))
                for mask in masks:
                    in_flight[k, share, mask, piece].wait_recv()
                top = (pieces - piece) * size
                bottom = top - size
                leaving = []
                if k + 1 < n_stages:
                    next_bits, next_stay, next_pieces, next_size = plans[share][k + 1]
                    for mask in reversed(range(1, 2 ** len(next_bits))):
                        for next_piece in range(next_pieces):
                            low = mask * next_stay + (next_pieces - 1 - next_piece) * next_size
                            if bottom <= low < top:
                                leaving.append((low, low + next_size, mask, next_piece))
                for low, high, mask, next_piece in leaving:
                    for m in masks:
                        absorb(k, share, m, piece, low, high)
                    forward(k + 1, share, mask, next_piece)
                rest = min([low for low, *_ in leaving] + [top])
                if rest > bottom:
                    for m in masks:
                        absorb(k, share, m, piece, bottom, rest)

    for share, (start, length) in enumerate(SHARES):
        total = work[share][0] + own_ref[start : start + length, :]
        work[share][0] = jnp.maximum(total, 0.0)
    hid_own[...] = jnp.concatenate([work[share][0] for share in range(n_shares)], axis=0).astype(jnp.bfloat16)

    def to_pair(src, dst, number):
        return pltpu.make_async_remote_copy(
            src_ref=src,
            dst_ref=dst,
            send_sem=pair_sem.at[0, number],
            recv_sem=pair_sem.at[1, number],
            device_id={"feat": 1 - f},
            device_id_type=MESH,
        )

    share_hidden = to_pair(hid_own, hid_other, 0)
    share_hidden.start()
    share_hidden.wait()
    mine, theirs = hid_own[...], hid_other[...]
    hidden = jnp.concatenate([jnp.where(f == 0, mine, theirs), jnp.where(f == 0, theirs, mine)], axis=0)
    width = hidden.shape[1] // 2
    def to_receiver(i):
        return pltpu.make_async_remote_copy(
            src_ref=rows_out.at[i],
            dst_ref=rows_in.at[me],
            send_sem=rows_sem.at[0],
            recv_sem=rows_sem.at[1],
            device_id={"dom": receivers[i]},
            device_id_type=MESH,
        )

    near = nx * ny
    for first in list(range(near, len(receivers), near)) + [0]:
        picked = jnp.dot(
            onehot[first * slots : (first + near) * slots, :], hidden, preferred_element_type=jnp.float32
        )
        for i in range(first, first + near):
            block = picked[(i - first) * slots : (i - first + 1) * slots, :]
            rows_out[i] = jnp.concatenate([block[:, :width], block[:, width:]], axis=0).astype(jnp.bfloat16)
        for i in range(max(first, 1), first + near):
            to_receiver(i).start()

    @pl.when(f == 0)
    def _():
        rows_in[me] = rows_out[0]

    @pl.when(f == 1)
    def _():
        to_receiver(0).start()

    n_own = hidden.shape[0]
    out_rows = out_ref.shape[0]
    own_total = jnp.dot(adj_ref[:, :n_own], hidden, preferred_element_type=jnp.float32)
    self_logits = lax.dot_general(
        hidden[:out_rows], w_self_ref[...], (((1,), (1,)), ((), ())), preferred_element_type=jnp.float32
    )
    blocks = len(receivers)

    def wait_rows(n):
        for number, ref in ((0, rows_out), (1, rows_in)):
            pltpu.make_async_copy(ref.at[pl.ds(0, n)], ref.at[pl.ds(0, n)], rows_sem.at[number]).wait()

    pl.when(f == 0)(lambda: wait_rows(blocks - 1))
    pl.when(f == 1)(lambda: wait_rows(blocks))

    arrived = rows_in[...].astype(jnp.float32)
    pool = [
        arrived[:, k * slots : (k + 1) * slots, :].reshape(parts * slots, width).astype(jnp.bfloat16)
        for k in range(2)
    ]
    share_part = []
    for k in range(2):
        part[:, k * width : (k + 1) * width] = jnp.dot(
            adj_ref[:, n_own:], pool[k], preferred_element_type=jnp.float32
        )
        at = (slice(None), pl.ds(k * width, width))
        share_part.append(to_pair(part.at[at], part_other.at[at], 1 + k))
        share_part[k].start()
    for copy in share_part:
        copy.wait()
    aggregate = (part[...] + part_other[...] + own_total).astype(jnp.bfloat16)
    out_ref[...] = self_logits + lax.dot_general(
        aggregate, w_neigh_ref[...], (((1,), (1,)), ((), ())), preferred_element_type=jnp.float32
    )
    for copy in in_flight.values():
        copy.wait_send()


def second_layer(parts, keeps, own, lists, counts, adj, w_self, w_neigh):
    plans = [plan_of(parts, share) for share in range(len(SHARES))]
    n_stages = len(plans[0])
    whole = pl.BlockSpec(memory_space=pltpu.VMEM)
    anywhere = pl.BlockSpec(memory_space=pl.ANY)
    rows, width = own.shape
    half = width // 2
    lengths = [length for _, length in SHARES]
    slots = lists.shape[1]
    buffers = [pltpu.VMEM((parts // 2,) + a.shape[1:], jnp.float32) for a in keeps]
    for first_stage in (None, 0, 1):
        for k in range(1) if first_stage is None else range(first_stage, n_stages):
            for share, n in enumerate(lengths):
                bits, stay, pieces, size = plans[share][k]
                buffers.append(pltpu.VMEM(((2 ** len(bits) - 1) * pieces, size * n + size, half), jnp.int32))
    chunk = max(chunk_of(parts), 8)
    buffers += [pltpu.VMEM((chunk, half), jnp.float32)] * 3
    buffers += [
        pltpu.VMEM(lists.shape[1:], jnp.int32),
        pltpu.VMEM((parts // 2 * slots, 2 * rows), jnp.bfloat16),
        pltpu.VMEM((rows, width), jnp.bfloat16),
        pltpu.VMEM((rows, width), jnp.bfloat16),
        pltpu.VMEM((parts // 2, 2 * slots, half), jnp.bfloat16),
        pltpu.VMEM((parts, 2 * slots, half), jnp.bfloat16),
        pltpu.VMEM((adj.shape[0], width), jnp.float32),
        pltpu.VMEM((adj.shape[0], width), jnp.float32),
        pltpu.VMEM(counts.shape, counts.dtype),
        pltpu.VMEM(adj.shape, adj.dtype),
        pltpu.VMEM(w_self.shape, w_self.dtype),
        pltpu.VMEM(w_neigh.shape, w_neigh.dtype),
    ]
    numbers = max(sum((2 ** len(p[0]) - 1) * p[2] for p in plan) for plan in plans)
    dma = pltpu.SemaphoreType.DMA
    buffers += [
        dma((len(SHARES) + 5,)),
        dma((len(SHARES), numbers)),
        dma((len(SHARES), numbers)),
        dma((2, 3)),
        dma((2,)),
    ]
    return pl.pallas_call(
        functools.partial(second_layer_kernel, parts),
        out_shape=jax.ShapeDtypeStruct((adj.shape[0], w_self.shape[0]), jnp.float32),
        in_specs=[whole] * 4 + [anywhere] * 5,
        out_specs=whole,
        scratch_shapes=buffers,
        compiler_params=pltpu.CompilerParams(
            collective_id=1, has_side_effects=True, vmem_limit_bytes=SECOND_VMEM
        ),
        name="reduce_and_second_layer",
    )(*keeps, own, lists, counts, adj, w_self, w_neigh)


def body(
    features,
    tile_weight,
    tile_dst,
    tile_src,
    tile_rows,
    w_self1,
    neighbour_weight_first,
    send_list,
    send_count,
    adj_two,
    w_self2,
    w_neigh2,
):
    parts = lax.axis_size("dom")
    other, wn_other, ws_other = swap(features, neighbour_weight_first, w_self1)
    results = first_layer(
        parts,
        tile_dst,
        tile_src,
        tile_rows,
        features,
        other,
        neighbour_weight_first,
        wn_other,
        w_self1,
        ws_other,
        tile_weight,
    )
    return second_layer(parts, results[:3], results[3], send_list.transpose(0, 2, 1), send_count, adj_two, w_self2.T, w_neigh2.T)


def solution(mesh):
    in_specs = (
        P("dom", "feat"),
        P("dom", None, None),
        P("dom"),
        P("dom"),
        P("dom"),
        P("feat", None),
        P("feat", None),
        P(),
        P(),
        P("dom", None),
        P(),
        P(),
    )
    out_specs = P("dom", None)
    return jax.shard_map(body, mesh=mesh, in_specs=in_specs, out_specs=out_specs, check_vma=False)
```
